128 devices in a mesh: ctx: 16 (over x, y), head: 8 (over z, core).
Axes of the slice: x: 4, y: 4, z: 4, core: 2. Of those that a mesh axis runs over, the one named last changes fastest.
Arguments:
- queries: bfloat16 [10240, 32, 128], P('ctx', 'head'), may hold values from -8 to 8
- key_rows: bfloat16 [10240, 32, 128], P('ctx', 'head'), may hold values from -8 to 8
- value_rows: bfloat16 [10240, 32, 128], P('ctx', 'head'), may hold values from -6 to 6
- out_weight: bfloat16 [32, 128, 4096], P('head'), may hold values from -0.09375 to 0.09375
- out_grad: bfloat16 [10240, 4096], P('ctx', 'head'), may hold values from -6 to 6
- global_ids: int32 [2], replicated, may hold values from 0 to 159, as said below
- random_ids: int32 [160, 3], replicated, may hold values from 0 to 159, as said below
- random_count: int32 [160], replicated, may hold values from 1 to 3
Outputs:
- projected: bfloat16 [10240, 4096], P('ctx', 'head')
- query_grad: bfloat16 [10240, 32, 128], P('ctx', 'head')
- key_grad: bfloat16 [10240, 32, 128], P('ctx', 'head')
- value_grad: bfloat16 [10240, 32, 128], P('ctx', 'head')
The draws below stay inside these ranges and needn't reach their ends.
Inputs may be any that keep to these rules, and one draw needn't show every extreme that they name: `global_ids`: 2 distinct block numbers; the last block is one of them. `random_ids`: block numbers; padded slots hold block numbers too. The 30 entries of the query blocks of one index of ctx (blocks k * 10 to k * 10 + 9) name blocks held by any one index at most 3 times, and in every draw some index is named exactly 3 times by the entries of every index.
All inputs are finite; a program needn't handle non-finite values.
Results may differ from the reference program's by a relative error of at most 0.03.
Values may be sent and summed in bfloat16 or wider, within the bound.
A program may use at most 192 MiB of HBM per device.

```python
import math
import jax
import jax.numpy as jnp
from jax import lax

HEADS = 32
HD = 128
DOUT = 4096
BLOCK = 64
G = 2
R = 3
NBD = 10
TOKENS = 10240
NB = 160
CAP = 3


def draw_queries(key, part):
    key = jax.random.fold_in(key, 1)
    drawn = jnp.clip(jax.random.normal(key, (TOKENS, HEADS, HD), jnp.float32), -8.0, 8.0)
    return drawn.astype(jnp.bfloat16)


def draw_key_rows(key, part):
    key = jax.random.fold_in(key, 2)
    drawn = jnp.clip(jax.random.normal(key, (TOKENS, HEADS, HD), jnp.float32), -8.0, 8.0)
    return drawn.astype(jnp.bfloat16)


def draw_global_ids(key, part):
    key = jax.random.fold_in(key, 3)
    key_pick, key_order = jax.random.split(key)
    others = jax.random.permutation(key_pick, NB - 1)[:G - 1].astype(jnp.int32)
    chosen = jnp.concatenate([others, jnp.full((1,), NB - 1, jnp.int32)])
    return jax.random.permutation(key_order, chosen).astype(jnp.int32)


def draw_random_ids(key, part):
    key = jax.random.fold_in(key, 4)
    owners_total = NB // NBD
    slot_total = NBD * R
    key_hot, key_rest = jax.random.split(key)
    hot_owner = jax.random.randint(key_hot, (), 0, owners_total).astype(jnp.int32)

    def one_source(source_key):
        key_pick, key_mix, key_local = jax.random.split(source_key, 3)
        tickets = jnp.repeat(jnp.arange(owners_total - 1, dtype=jnp.int32), CAP)
        chosen = jax.random.permutation(key_pick, tickets)[:slot_total - CAP]
        others = chosen + (chosen >= hot_owner).astype(jnp.int32)
        owners = jnp.concatenate([jnp.full((CAP,), hot_owner, jnp.int32), others])
        owners = jax.random.permutation(key_mix, owners)
        local_block = jax.random.randint(key_local, (slot_total,), 0, NBD).astype(jnp.int32)
        return (owners * NBD + local_block).reshape(NBD, R)
    drawn = jax.vmap(one_source)(jax.random.split(key_rest, owners_total))
    return drawn.reshape(NB, R).astype(jnp.int32)


def draw_random_count(key, part):
    key = jax.random.fold_in(key, 5)
    key_counts, key_spots = jax.random.split(key)
    drawn = jax.random.randint(key_counts, (NB,), 1, R + 1).astype(jnp.int32)
    picked_rows = jax.random.permutation(key_spots, NB)
    drawn = drawn.at[picked_rows[0]].set(R).at[picked_rows[1]].set(1)
    return drawn.astype(jnp.int32)


def block_scale(rng, extent, cuts, smallest, top_value):
    factor_of = 1.0
    for position, parts in cuts:
        draws = jax.random.uniform(jax.random.fold_in(jax.random.fold_in(rng, 6), position), (parts,), jnp.float32, smallest / len(cuts), top_value / len(cuts))
        factor_of = factor_of * jnp.repeat(jnp.exp(draws), extent[position] // parts).reshape((-1,) + (1,) * (len(extent) - 1 - position))
    return factor_of


def scatter_about(stream_key, shape, width, limit, cuts=(), kind=jnp.bfloat16):
    entries = jax.random.normal(stream_key, shape, jnp.float32) * width
    if len(cuts) > 0:
        entries = block_scale(stream_key, shape, cuts, -0.22, 0.18) * entries
    return jnp.clip(entries, min=-limit, max=limit).astype(kind)


def setup_inputs(seed: int = 0) -> dict:
    streams_of = jax.random.split(jax.random.key(seed), 9)
    queries = draw_queries(jax.random.fold_in(streams_of[8], 71), 0)
    key_rows = draw_key_rows(jax.random.fold_in(streams_of[8], 71), 0)
    value_rows = scatter_about(streams_of[2], (TOKENS, HEADS, HD), 1.0, 6.0, ((0, 16), (1, 8)))
    out_weight = scatter_about(streams_of[3], (HEADS, HD, DOUT), (HEADS * HD) ** -0.5, 0.09375, ((0, 8),))
    out_grad = scatter_about(streams_of[4], (TOKENS, DOUT), 1.0, 6.0, ((0, 16), (1, 8)))
    global_ids = draw_global_ids(jax.random.fold_in(streams_of[8], 71), 0)
    random_ids = draw_random_ids(jax.random.fold_in(streams_of[8], 71), 0)
    random_count = draw_random_count(jax.random.fold_in(streams_of[8], 71), 0)
    return {"queries": queries, "key_rows": key_rows, "value_rows": value_rows, "out_weight": out_weight, "out_grad": out_grad, "global_ids": global_ids, "random_ids": random_ids, "random_count": random_count}


def key_lists(global_ids, random_ids, random_count):
    block_total = random_ids.shape[0]
    row_ids = jnp.arange(block_total, dtype=jnp.int32)
    window = row_ids[:, None] + jnp.arange(-1, 2, dtype=jnp.int32)[None, :]
    window_ok = (window >= 0) & (window < block_total)
    window = jnp.clip(window, 0, block_total - 1).astype(jnp.int32)
    global_cols = jnp.broadcast_to(global_ids.astype(jnp.int32)[None, :], (block_total, G))
    random_ok = jnp.arange(R, dtype=jnp.int32)[None, :] < random_count[:, None]
    block_ids = jnp.concatenate([window, global_cols, random_ids.astype(jnp.int32)], axis=1)
    valid_mask = jnp.concatenate([window_ok, jnp.ones((block_total, G), dtype=bool), random_ok], axis=1)
    return (block_ids, valid_mask)

def reference(queries, key_rows, value_rows, out_weight, out_grad, global_ids, random_ids, random_count):
    score_scale = 1.0 / math.sqrt(HD)
    local_count = 3 + G
    block_ids, valid_mask = key_lists(global_ids, random_ids, random_count)
    query_blocks = queries.reshape(NB, BLOCK, HEADS, HD)
    key_blocks = key_rows.reshape(NB, BLOCK, HEADS, HD)
    value_blocks = value_rows.reshape(NB, BLOCK, HEADS, HD)
    weight_flat = out_weight.reshape(HEADS * HD, DOUT)
    grad_blocks = out_grad.reshape(NB, BLOCK, DOUT)

    def one_block(running, inputs):
        key_total, value_total = running
        query_block, grad_block, listed_ids, listed_ok = inputs
        key_chosen = key_blocks[listed_ids].astype(jnp.float32)
        value_chosen = value_blocks[listed_ids].astype(jnp.float32)
        query_wide = query_block.astype(jnp.float32)
        scores = jnp.einsum('qhd,skhd->hqsk', query_wide, key_chosen) * score_scale
        scores = jnp.where(listed_ok[None, None, :, None], scores, -jnp.inf)
        row_peak = lax.optimization_barrier(jnp.max(scores, axis=(2, 3), keepdims=True))
        weights_raw = jnp.exp(scores - row_peak)
        probabilities = weights_raw / lax.optimization_barrier(jnp.sum(weights_raw, axis=(2, 3), keepdims=True))
        probs_low = probabilities.astype(jnp.bfloat16)
        attended = jnp.einsum('hqsk,skhd->qhd', probs_low.astype(jnp.float32), value_chosen).astype(jnp.bfloat16)
        out_block = jnp.dot(attended.reshape(BLOCK, HEADS * HD), weight_flat, preferred_element_type=jnp.float32).astype(jnp.bfloat16)
        attended_grad = jnp.dot(grad_block, weight_flat.T, preferred_element_type=jnp.float32).astype(jnp.bfloat16).reshape(BLOCK, HEADS, HD)
        grad_wide = attended_grad.astype(jnp.float32)
        row_delta = lax.optimization_barrier(jnp.sum(grad_wide * attended.astype(jnp.float32), axis=2))
        prob_grad = jnp.einsum('qhd,skhd->hqsk', grad_wide, value_chosen)
        score_grad = (probabilities * (prob_grad - row_delta.T[:, :, None, None])).astype(jnp.bfloat16)
        score_wide = score_grad.astype(jnp.float32)
        query_part = (jnp.einsum('hqsk,skhd->qhd', score_wide, key_chosen) * score_scale).astype(jnp.bfloat16)
        key_part = jnp.einsum('hqsk,qhd->skhd', score_wide, query_wide) * score_scale
        value_part = jnp.einsum('hqsk,qhd->skhd', probs_low.astype(jnp.float32), grad_wide)
        rounded = lax.optimization_barrier((key_part[local_count:].astype(jnp.bfloat16), value_part[local_count:].astype(jnp.bfloat16)))
        key_part = jnp.concatenate([key_part[:local_count], rounded[0].astype(jnp.float32)], axis=0)
        value_part = jnp.concatenate([value_part[:local_count], rounded[1].astype(jnp.float32)], axis=0)
        key_total = key_total.at[listed_ids].add(key_part)
        value_total = value_total.at[listed_ids].add(value_part)
        return ((key_total, value_total), (out_block, query_part))
    start_sums = (jnp.zeros((NB, BLOCK, HEADS, HD), jnp.float32), jnp.zeros((NB, BLOCK, HEADS, HD), jnp.float32))
    totals, outputs = lax.scan(one_block, start_sums, (query_blocks, grad_blocks, block_ids, valid_mask))
    projected = outputs[0].reshape(TOKENS, DOUT)
    query_grad = outputs[1].reshape(TOKENS, HEADS, HD)
    key_grad = totals[0].reshape(TOKENS, HEADS, HD).astype(jnp.bfloat16)
    value_grad = totals[1].reshape(TOKENS, HEADS, HD).astype(jnp.bfloat16)
    return (projected, query_grad, key_grad, value_grad)
```

```python
import functools
import math

import jax
import jax.numpy as jnp
from jax import lax
from jax.experimental import pallas as pl
from jax.experimental.pallas import tpu as pltpu
from jax.sharding import PartitionSpec as P

SIDE = 4
BLOCK = 64
G = 2
R = 3
HERE = 640
NBD = 10
HD = 128
HPD = 4
NB = 160
SHARD = 512
MESH = pl.DeviceIdType.MESH
NT = (((1,), (1,)), ((), ()))
TN = (((0,), (0,)), ((), ()))
DZ = (1, 3, 2)


def place():
    ctx, hd = lax.axis_index("ctx"), lax.axis_index("head")
    return ctx, hd, ctx // SIDE, lax.rem(ctx, SIDE), hd // 2, lax.rem(hd, 2)


def query_row(y, c):
    return y * (1 - c) + (3 - y) * c


def remote(src, dst, send, recv, device):
    return pltpu.make_async_remote_copy(
        src_ref=src, dst_ref=dst, send_sem=send, recv_sem=recv, device_id=device, device_id_type=MESH
    )


def greet(device):
    pl.semaphore_signal(pltpu.get_barrier_semaphore(), inc=1, device_id=device, device_id_type=MESH)


def rows_of(index):
    return pl.ds(pl.multiple_of(index * HERE, HERE), HERE)


def gather_kernel(
    kvq, og, w, ka, va, qa, doa,
    ogv, acc, dov,
    ks, kr, fs, fr, qs, qr, ds, dr, zs, zr, cs, cr, own,
):
    ctx, hd, x, y, z, c = place()
    half = y // 2
    other = {"head": 2 * z + 1 - c}
    cw = lax.rem(half + c, 2)
    yw = query_row(y, cw)
    src_half = lax.rem(half + c, 2)
    other_half = lax.rem(half + 1 - c, 2)
    ys = query_row(y, c)
    to_self = 1 - jnp.minimum(c + half, 1)

    def worker(k, b):
        return {"ctx": k * SIDE + 2 * c + b, "head": 2 * z + cw}

    def query_worker(k):
        return {"ctx": k * SIDE + yw, "head": 2 * z + cw}

    def source(xs, t):
        return {"ctx": xs * SIDE + 2 * src_half + t, "head": 2 * z + half}

    for dx in range(SIDE):
        xs = lax.rem(x + dx, SIDE)
        for t in range(2):
            if dx:
                greet(source(xs, t))
            else:
                mine = (2 * src_half + t == y) & (half == c)

                @pl.when(jnp.logical_not(mine))
                def _():
                    greet(source(xs, t))
    for dz in DZ:
        greet({"head": 2 * lax.rem(z + dz, SIDE) + c})
    greet(other)
    pl.semaphore_wait(pltpu.get_barrier_semaphore(), 12 - to_self)

    local = pltpu.make_async_copy(og, ogv.at[hd], own)
    local.start()
    core = [remote(og, ogv.at[hd], cs.at[0], cr.at[0], other)]
    core[0].start()
    sends = []
    for i, dz in ((2, 2), (0, 1), (1, 3)):
        for q in range(4):
            part = pl.ds(q * 160, 160)
            copy = remote(
                og.at[part], ogv.at[hd, part], zs.at[i, q], zr.at[i, q],
                {"head": 2 * lax.rem(z + dz, SIDE) + c},
            )
            copy.start()
            sends.append(copy)

    slot = x * 2 + lax.rem(y, 2)
    own_sends = []
    for dx in (2, 1, 3, 0):
        k = lax.rem(x + dx, SIDE)
        for t, dst in ((0, ka), (1, va)):
            for b in range(2):
                copy = remote(
                    kvq.at[k, t], dst.at[rows_of(ctx)], ks.at[dx, b, t], kr.at[slot, t], worker(k, b)
                )
                if dx:
                    copy.start()
                    sends.append(copy)
                else:
                    mine = (2 * c + b == y) & (cw == c)
                    here = pltpu.make_async_copy(kvq.at[k, t], dst.at[rows_of(ctx)], kr.at[slot, t])
                    pl.when(jnp.logical_not(mine))(copy.start)
                    pl.when(mine)(here.start)
                    own_sends.append((copy, mine))
    for dx in (2, 1, 3, 0):
        k = lax.rem(x + dx, SIDE)
        copy = remote(kvq.at[k, 2], qa.at[rows_of(x)], qs.at[dx], qr.at[x], query_worker(k))
        if dx:
            copy.start()
            sends.append(copy)
        else:
            mine = (yw == y) & (cw == c)
            here = pltpu.make_async_copy(kvq.at[k, 2], qa.at[rows_of(x)], qr.at[x])
            pl.when(jnp.logical_not(mine))(copy.start)
            pl.when(mine)(here.start)
            own_sends.append((copy, mine))

    acc[...] = jnp.zeros_like(acc)

    def add_shard(s):
        columns = pl.ds(pl.multiple_of(s * SHARD, SHARD), SHARD)

        def tile(i, carry):
            part = pl.ds(pl.multiple_of(i * 128, 128), 128)
            acc[part, :] += lax.dot_general(
                ogv[s, part, :], w[:, columns], NT, preferred_element_type=jnp.float32
            )
            return carry

        lax.fori_loop(0, HERE // 128, tile, 0)

    def forward(j):
        xs, t2 = j // 2, j % 2
        idx = xs * SIDE + 2 * src_half + t2
        for t, dst in ((0, ka), (1, va)):
            part = dst.at[rows_of(idx)]
            remote(part, part, fs.at[j, t], kr.at[j, t], other).wait_recv()
            copy = remote(part, part, fs.at[j, t], fr.at[j, t], other)
            copy.start()
            sends.append(copy)

    local.wait()
    add_shard(hd)
    core[0].wait_recv()
    add_shard(2 * z + 1 - c)
    for i in range(3):
        zp = lax.rem(z + SIDE - DZ[i], SIDE)
        s = 2 * zp + c
        for q in range(4):
            part = pl.ds(q * 160, 160)
            view = ogv.at[s, part]
            remote(view, view, zs.at[i, q], zr.at[i, q], other).wait_recv()
        copy = remote(ogv.at[s], ogv.at[s], cs.at[1 + i], cr.at[1 + i], other)
        copy.start()
        core.append(copy)
        add_shard(s)
    for i in range(3):
        zp = lax.rem(z + SIDE - DZ[i], SIDE)
        core[1 + i].wait_recv()
        add_shard(2 * zp + 1 - c)
    for k in range(HPD):
        dov[k] = acc[:, k * HD : (k + 1) * HD].astype(jnp.bfloat16)
    for dx in (2, 1, 3, 0):
        k = lax.rem(x + dx, SIDE)
        copy = remote(dov.at[k], doa.at[rows_of(x)], ds.at[dx], dr.at[x], query_worker(k))
        if dx:
            copy.start()
            sends.append(copy)
        else:
            mine = (yw == y) & (cw == c)
            here = pltpu.make_async_copy(dov.at[k], doa.at[rows_of(x)], dr.at[x])
            pl.when(jnp.logical_not(mine))(copy.start)
            pl.when(mine)(here.start)
            own_sends.append((copy, mine))
    for j in range(8):
        forward(j)
    for xs in range(SIDE):
        part = qa.at[rows_of(xs)]
        remote(part, part, qs.at[0], qr.at[xs], other).wait_recv()
        part = doa.at[rows_of(xs)]
        remote(part, part, ds.at[0], dr.at[xs], other).wait_recv()
    for j in range(8):
        idx = (j // 2) * SIDE + 2 * other_half + j % 2
        for t, dst in ((0, ka), (1, va)):
            part = dst.at[rows_of(idx)]
            remote(part, part, fs.at[j, t], fr.at[j, t], other).wait_recv()
    for copy in sends + core:
        copy.wait_send()
    for copy, mine in own_sends:
        pl.when(jnp.logical_not(mine))(copy.wait_send)


def attention_kernel(rid, rcnt, gid, q, do, k, v, o, dq, dk, dv, dka, dva, dkg, dvg):
    ctx, hd, x, y, z, c = place()
    ys = query_row(y, c)
    scale = 1.0 / math.sqrt(HD)
    f32 = jnp.float32
    dka[...] = jnp.zeros_like(dka)
    dva[...] = jnp.zeros_like(dva)
    dkg[...] = jnp.zeros_like(dkg)
    dvg[...] = jnp.zeros_like(dvg)

    def span(block, count):
        return pl.ds(pl.multiple_of(block * BLOCK, BLOCK), count * BLOCK)

    g0, g1 = span(gid[0], 1), span(gid[1], 1)
    column = lax.broadcasted_iota(jnp.int32, (1, 8 * BLOCK), 1) // BLOCK

    def step(n, carry):
        xs = n // NBD
        i = (xs * SIDE + ys) * NBD + (n - xs * NBD)
        first = jnp.clip(i - 1, 0, NB - 3)
        window = span(first, 3)
        randoms = [span(rid[i * R + r], 1) for r in range(R)]
        count = rcnt[i]
        kc = jnp.concatenate([k[window, :], k[g0, :], k[g1, :]] + [k[r, :] for r in randoms], axis=0)
        vc = jnp.concatenate([v[window, :], v[g0, :], v[g1, :]] + [v[r, :] for r in randoms], axis=0)
        mine = span(n, 1)
        qn, dn = q[mine, :], do[mine, :]
        low, high = i - 1 - first, i + 1 - first
        keep = ((column >= low) & (column <= high)) | ((column >= 3) & (column < 5 + count))
        keep = keep & ((column <= high) | (column >= 3))
        s = lax.dot_general(qn, kc, NT, preferred_element_type=f32) * scale
        s = jnp.where(keep, s, -1e30)
        peak = jnp.max(s, axis=1, keepdims=True)
        e = jnp.exp(s - peak)
        p = e / jnp.sum(e, axis=1, keepdims=True)
        low_p = p.astype(jnp.bfloat16)
        on = jnp.dot(low_p, vc, preferred_element_type=f32).astype(jnp.bfloat16)
        o[mine, :] = on
        delta = jnp.sum(dn.astype(f32) * on.astype(f32), axis=1, keepdims=True)
        dp = lax.dot_general(dn, vc, NT, preferred_element_type=f32)
        dsc = (p * (dp - delta)).astype(jnp.bfloat16)
        dq[mine, :] = (jnp.dot(dsc, kc, preferred_element_type=f32) * scale).astype(jnp.bfloat16)
        dkt = lax.dot_general(dsc, qn, TN, preferred_element_type=f32)
        dvt = lax.dot_general(low_p, dn, TN, preferred_element_type=f32)
        for total, glob, term in ((dka, dkg, dkt), (dva, dvg, dvt)):
            total[window, :] += term[: 3 * BLOCK]
            glob[...] += term[3 * BLOCK : 5 * BLOCK]
            for r in range(R):
                total[randoms[r], :] += term[(5 + r) * BLOCK : (6 + r) * BLOCK]
        return carry

    lax.fori_loop(0, 4 * NBD, step, 0)
    for total, glob in ((dka, dkg), (dva, dvg)):
        total[g0, :] += glob[:BLOCK]
        total[g1, :] += glob[BLOCK:]

    def finish(n, carry):
        part = pl.ds(pl.multiple_of(n * 256, 256), 256)
        dk[part, :] = (dka[part, :] * scale).astype(jnp.bfloat16)
        dv[part, :] = dva[part, :].astype(jnp.bfloat16)
        return carry

    lax.fori_loop(0, NB * BLOCK // 256, finish, 0)


def return_kernel(
    oa, dqa, dka, dva, w, proj, dqh, dkh, dvh,
    oh, part_out, core_in, z_in, last, dmine, dcore, dhome,
    os, orr, qs, qr, es, er, ls, hs, hr, cs, cr, zs, zr,
):
    ctx, hd, x, y, z, c = place()
    f32 = jnp.float32
    half = y // 2
    other = {"head": 2 * z + 1 - c}
    cw = lax.rem(half + c, 2)
    src_half = lax.rem(half + c, 2)
    other_half = lax.rem(half + 1 - c, 2)
    ys = query_row(y, c)
    to_self = 1 - jnp.minimum(c + half, 1)

    def home(xs, yy):
        return {"ctx": xs * SIDE + yy, "head": 2 * z + half}

    def worker(k, b):
        return {"ctx": k * SIDE + 2 * c + b, "head": 2 * z + cw}

    for dx in range(SIDE):
        k = lax.rem(x + dx, SIDE)
        for b in range(2):
            if dx:
                greet(worker(k, b))
            else:
                mine = (2 * c + b == y) & (cw == c)

                @pl.when(jnp.logical_not(mine))
                def _():
                    greet(worker(k, b))
    for dz in DZ:
        greet({"head": 2 * lax.rem(z + dz, SIDE) + c})
    greet(other)
    pl.semaphore_wait(pltpu.get_barrier_semaphore(), 12 - to_self)

    sends, own_sends = [], []

    def send_home(src, dst, send, recv, dx, yy):
        copy = remote(src, dst, send, recv, home(lax.rem(x + dx, SIDE), yy))
        if dx:
            copy.start()
            sends.append(copy)
        else:
            mine = (yy == y) & (half == c)
            here = pltpu.make_async_copy(src, dst, recv)
            pl.when(jnp.logical_not(mine))(copy.start)
            pl.when(mine)(here.start)
            own_sends.append((copy, mine))

    for dx in (2, 1, 3, 0):
        xs = lax.rem(x + dx, SIDE)
        send_home(oa.at[rows_of(xs)], oh.at[x], os.at[dx], orr.at[x], dx, ys)
    loads = []
    for j in range(8):
        idx = (j // 2) * SIDE + 2 * other_half + j % 2
        mid = (j // 2) * SIDE + 2 * src_half + j % 2
        for t, src in ((0, dka), (1, dva)):
            copy = remote(src.at[rows_of(idx)], dcore.at[j, t], es.at[j, t], er.at[j, t], other)
            copy.start()
            sends.append(copy)
            copy = pltpu.make_async_copy(src.at[rows_of(mid)], dmine.at[j, t], ls.at[j, t])
            copy.start()
            loads.append(copy)
    for dx in (2, 1, 3, 0):
        xs = lax.rem(x + dx, SIDE)
        send_home(dqa.at[rows_of(xs)], dqh.at[x], qs.at[dx], qr.at[x], dx, ys)

    b = lax.rem(y, 2)
    for dx in (2, 1, 3, 0):
        xs = lax.rem(x + dx, SIDE)
        for t2 in range(2):
            j = xs * 2 + t2
            for t in range(2):
                pltpu.make_async_copy(dmine.at[j, t], dmine.at[j, t], ls.at[j, t]).wait()
                remote(dcore.at[j, t], dcore.at[j, t], es.at[j, t], er.at[j, t], other).wait_recv()
                dmine[j, t] = (dmine[j, t].astype(f32) + dcore[j, t].astype(f32)).astype(jnp.bfloat16)
                send_home(
                    dmine.at[j, t], dhome.at[x, b, t], hs.at[dx, t2, t], hr.at[x, b, t],
                    dx, 2 * src_half + t2,
                )

    for k in range(HPD):
        remote(oh.at[k], oh.at[k], os.at[0], orr.at[k], other).wait_recv()

    def shard_product(s, put):
        columns = pl.ds(pl.multiple_of(s * SHARD, SHARD), SHARD)

        def tile(i, carry):
            part = pl.ds(pl.multiple_of(i * 128, 128), 128)
            rows = jnp.concatenate([oh[k, part, :] for k in range(HPD)], axis=1)
            put(part, jnp.dot(rows, w[:, columns], preferred_element_type=f32))
            return carry

        lax.fori_loop(0, HERE // 128, tile, 0)

    for i, dz in enumerate((2, 1, 3, 0)):
        zp = lax.rem(z + dz, SIDE)

        def put(part, value):
            part_out[i, part, :] = value.astype(jnp.bfloat16)

        shard_product(2 * zp + 1 - c, put)
        copy = remote(part_out.at[i], core_in.at[i], cs.at[i], cr.at[i], other)
        copy.start()
        sends.append(copy)
    for i, dz in enumerate((2, 1, 3)):
        zp = lax.rem(z + dz, SIDE)
        remote(core_in.at[i], core_in.at[i], cs.at[i], cr.at[i], other).wait_recv()

        def put(part, value):
            part_out[4 + i, part, :] = (value + core_in[i, part, :].astype(f32)).astype(jnp.bfloat16)

        shard_product(2 * zp + c, put)
        copy = remote(part_out.at[4 + i], z_in.at[i], zs.at[i], zr.at[i], {"head": 2 * zp + c})
        copy.start()
        sends.append(copy)
    remote(core_in.at[3], core_in.at[3], cs.at[3], cr.at[3], other).wait_recv()

    def put(part, value):
        last[part, :] = value + core_in[3, part, :].astype(f32)

    shard_product(hd, put)

    for k in range(HPD):
        for t, out in ((0, dkh), (1, dvh)):
            for bb in range(2):
                view = dhome.at[k, bb, t]
                remote(view, view, hs.at[0, 0, 0], hr.at[k, bb, t], other).wait_recv()
            out[k] = (dhome[k, 0, t].astype(f32) + dhome[k, 1, t].astype(f32)).astype(jnp.bfloat16)
    for i in range(3):
        remote(z_in.at[i], z_in.at[i], zs.at[i], zr.at[i], other).wait_recv()
        if i < 2:
            last[...] += z_in[i].astype(f32)
        else:
            proj[...] = (last[...] + z_in[i].astype(f32)).astype(jnp.bfloat16)
    for k in range(HPD):
        remote(dqh.at[k], dqh.at[k], qs.at[0], qr.at[k], other).wait_recv()
    for copy in sends:
        copy.wait_send()
    for copy, mine in own_sends:
        pl.when(jnp.logical_not(mine))(copy.wait_send)


ANY = pl.BlockSpec(memory_space=pl.ANY)
VMEM = pl.BlockSpec(memory_space=pltpu.VMEM)
SMEM = pl.BlockSpec(memory_space=pltpu.SMEM)
LIMIT = 56 * 1024 * 1024


def struct(*shape):
    return jax.ShapeDtypeStruct(shape, jnp.bfloat16)


def sem(*shape):
    return pltpu.SemaphoreType.DMA(shape)


def local(queries, key_rows, value_rows, out_weight, out_grad, global_ids, random_ids, random_count):
    bf16, f32 = jnp.bfloat16, jnp.float32
    kvq = jnp.transpose(jnp.stack([key_rows, value_rows, queries], axis=0), (2, 0, 1, 3))
    w = out_weight.reshape(HPD * HD, out_weight.shape[2])
    tokens = NB * BLOCK
    ka, va, qa, doa = pl.pallas_call(
        gather_kernel,
        out_shape=(struct(tokens, HD), struct(tokens, HD), struct(4 * HERE, HD), struct(4 * HERE, HD)),
        in_specs=[ANY, ANY, VMEM],
        out_specs=(ANY,) * 4,
        scratch_shapes=[
            pltpu.VMEM((8, HERE, SHARD), bf16),
            pltpu.VMEM((HERE, SHARD), f32),
            pltpu.VMEM((HPD, HERE, HD), bf16),
            sem(4, 2, 2), sem(8, 2), sem(8, 2), sem(8, 2), sem(4), sem(4), sem(4), sem(4),
            sem(3, 4), sem(3, 4), sem(4), sem(4), pltpu.SemaphoreType.DMA,
        ],
        compiler_params=pltpu.CompilerParams(
            collective_id=0, has_side_effects=True, vmem_limit_bytes=LIMIT
        ),
    )(kvq, out_grad, w)
    oa, dqa, dka, dva = pl.pallas_call(
        attention_kernel,
        out_shape=(struct(4 * HERE, HD), struct(4 * HERE, HD), struct(tokens, HD), struct(tokens, HD)),
        in_specs=[SMEM] * 3 + [VMEM] * 4,
        out_specs=(VMEM,) * 4,
        scratch_shapes=[
            pltpu.VMEM((tokens, HD), f32),
            pltpu.VMEM((tokens, HD), f32),
            pltpu.VMEM((2 * BLOCK, HD), f32),
            pltpu.VMEM((2 * BLOCK, HD), f32),
        ],
        compiler_params=pltpu.CompilerParams(vmem_limit_bytes=LIMIT),
    )(random_ids.reshape(NB * R), random_count, global_ids, qa, doa, ka, va)
    projected, dqh, dkh, dvh = pl.pallas_call(
        return_kernel,
        out_shape=(struct(HERE, SHARD),) + (struct(HPD, HERE, HD),) * 3,
        in_specs=[ANY] * 4 + [VMEM],
        out_specs=(VMEM, ANY, VMEM, VMEM),
        scratch_shapes=[
            pltpu.VMEM((HPD, HERE, HD), bf16),
            pltpu.VMEM((7, HERE, SHARD), bf16),
            pltpu.VMEM((4, HERE, SHARD), bf16),
            pltpu.VMEM((3, HERE, SHARD), bf16),
            pltpu.VMEM((HERE, SHARD), f32),
            pltpu.VMEM((8, 2, HERE, HD), bf16),
            pltpu.VMEM((8, 2, HERE, HD), bf16),
            pltpu.VMEM((HPD, 2, 2, HERE, HD), bf16),
            sem(4), sem(4), sem(4), sem(4), sem(8, 2), sem(8, 2), sem(8, 2),
            sem(4, 2, 2), sem(4, 2, 2), sem(4), sem(4), sem(3), sem(3),
        ],
        compiler_params=pltpu.CompilerParams(
            collective_id=1, has_side_effects=True, vmem_limit_bytes=LIMIT
        ),
    )(oa, dqa, dka, dva, w)
    grads = [jnp.transpose(g, (1, 0, 2)) for g in (dqh, dkh, dvh)]
    return (projected, *grads)


def solution(mesh):
    placed = (
        P("ctx", "head", None),
        P("ctx", "head", None),
        P("ctx", "head", None),
        P("head", None, None),
        P("ctx", "head"),
        P(),
        P(),
        P(),
    )
    return jax.shard_map(
        local,
        mesh=mesh,
        in_specs=placed,
        out_specs=(
            P("ctx", "head"),
            P("ctx", "head", None),
            P("ctx", "head", None),
            P("ctx", "head", None),
        ),
        check_vma=False,
    )
```

```python
import functools
import math

import jax
import jax.numpy as jnp
from jax import lax
from jax.experimental import pallas as pl
from jax.experimental.pallas import tpu as pltpu
from jax.sharding import PartitionSpec as P

SIDE = 4
BLOCK = 64
G = 2
R = 3
HERE = 640
NBD = 10
HD = 128
HPD = 4
NB = 160
SHARD = 512
MESH = pl.DeviceIdType.MESH
NT = (((1,), (1,)), ((), ()))
TN = (((0,), (0,)), ((), ()))


def place():
    ctx, hd = lax.axis_index("ctx"), lax.axis_index("head")
    return ctx, hd, ctx // SIDE, lax.rem(ctx, SIDE), hd // 2, lax.rem(hd, 2)


def query_row(y, c):
    return y * (1 - c) + (3 - y) * c


def remote(src, dst, send, recv, device):
    return pltpu.make_async_remote_copy(
        src_ref=src, dst_ref=dst, send_sem=send, recv_sem=recv, device_id=device, device_id_type=MESH
    )


def greet(device):
    pl.semaphore_signal(pltpu.get_barrier_semaphore(), inc=1, device_id=device, device_id_type=MESH)


def rows_of(index):
    return pl.ds(pl.multiple_of(index * HERE, HERE), HERE)


def neighbours(x, y, z, c):
    pair = {"ctx": x * SIDE + y + 1 - 2 * lax.rem(y, 2)}
    other = {"head": 2 * z + 1 - c}
    up = {"head": 2 * lax.rem(z + 1, SIDE) + c}
    down = {"head": 2 * lax.rem(z + 3, SIDE) + c}
    return pair, other, up, down


def enter(senders, to_self):
    for device, mine in senders:
        if mine is None:
            greet(device)
        else:
            pl.when(jnp.logical_not(mine))(functools.partial(greet, device))
    pl.semaphore_wait(pltpu.get_barrier_semaphore(), len(senders) - to_self)


class Sends:
    def __init__(self):
        self.started, self.guarded = [], []

    def start(self, copy):
        copy.start()
        self.started.append(copy)

    def start_unless(self, mine, src, dst, send, recv, device):
        copy = remote(src, dst, send, recv, device)
        here = pltpu.make_async_copy(src, dst, recv)
        pl.when(jnp.logical_not(mine))(copy.start)
        pl.when(mine)(here.start)
        self.guarded.append((copy, mine))

    def wait(self):
        for copy in self.started:
            copy.wait_send()
        for copy, mine in self.guarded:
            pl.when(jnp.logical_not(mine))(copy.wait_send)


QUARTER = HERE // 4


def quarter(q):
    return pl.ds(q * QUARTER, QUARTER)


def gather_kernel(
    kvq, og, w, ka, va, qa, doa,
    ogv, acc, dov,
    ks, kr, ps, pr, fs, fr, ds, dr, zs, zr, cs, cr, own,
):
    ctx, hd, x, y, z, c = place()
    half = y // 2
    pair, other, up, down = neighbours(x, y, z, c)
    cw = lax.rem(half + c, 2)
    yw = query_row(y, cw)
    py = y + 1 - 2 * lax.rem(y, 2)
    near, pair_near = query_row(y, c), query_row(py, c)
    other_near, other_pair_near = query_row(y, 1 - c), query_row(py, 1 - c)
    to_self = 1 - jnp.minimum(c + half, 1)
    me = to_self == 1

    def worker(k):
        return {"ctx": k * SIDE + yw, "head": 2 * z + cw}

    senders = [
        ({"ctx": lax.rem(x + dx, SIDE) * SIDE + near, "head": 2 * z + half}, None if dx else me)
        for dx in range(SIDE)
    ]
    enter(senders + [(up, None), (down, None), (other, None), (pair, None)], to_self)

    sends = Sends()

    def send_worker(src, dst, send, recv, dx, k):
        if dx:
            sends.start(remote(src, dst, send, recv, worker(k)))
        else:
            sends.start_unless(me, src, dst, send, recv, worker(k))

    def arrived(view, recv):
        remote(view, view, recv, recv, other).wait_recv()

    local = pltpu.make_async_copy(og, ogv.at[hd], own)
    local.start()
    for dx in (0, 1, 3, 2):
        k = lax.rem(x + dx, SIDE)
        for t, dst in ((0, ka), (1, va)):
            send_worker(kvq.at[k, t], dst.at[rows_of(ctx)], ks.at[dx, t], kr.at[x, t], dx, k)
        if dx == 0:
            for q in range(4):
                for i, to, p in ((0, up, q), (1, down, (q + 2) % 4)):
                    sends.start(
                        remote(og.at[quarter(p)], ogv.at[hd, quarter(p)], zs.at[i, p], zr.at[i, p], to)
                    )
            sends.start(remote(og, ogv.at[hd], cs.at[0], cr.at[0], other))
    for dx in (0, 1, 3, 2):
        k = lax.rem(x + dx, SIDE)
        send_worker(kvq.at[k, 2], qa.at[rows_of(x)], ks.at[dx, 2], kr.at[x, 2], dx, k)

    def add_shard(s):
        columns = pl.ds(pl.multiple_of(s * SHARD, SHARD), SHARD)

        def tile(i, carry):
            part = pl.ds(pl.multiple_of(i * 128, 128), 128)
            acc[part, :] += lax.dot_general(
                ogv[s, part, :], w[:, columns], NT, preferred_element_type=jnp.float32
            )
            return carry

        lax.fori_loop(0, HERE // 128, tile, 0)

    def pass_near(dx):
        xs = lax.rem(x + SIDE - dx, SIDE)
        for t, dst in ((0, ka), (1, va)):
            view = dst.at[rows_of(xs * SIDE + near)]
            arrived(view, kr.at[xs, t])
            sends.start(remote(view, view, ps.at[xs, t], pr.at[xs, t], pair))
            sends.start(remote(view, view, fs.at[xs, t], fr.at[xs, t], other))

    def pass_pair(dx):
        xs = lax.rem(x + SIDE - dx, SIDE)
        for t, dst in ((0, ka), (1, va)):
            view = dst.at[rows_of(xs * SIDE + pair_near)]
            arrived(view, pr.at[xs, t])
            sends.start(remote(view, view, fs.at[4 + xs, t], fr.at[4 + xs, t], other))

    below = 2 * lax.rem(z + 3, SIDE)
    above = 2 * lax.rem(z + 1, SIDE)
    across = 2 * lax.rem(z + 2, SIDE)

    pass_near(0)
    for q in range(2):
        for i, s, to, p in ((0, below, up, q), (1, above, down, q + 2)):
            view = ogv.at[s + c, quarter(p)]
            arrived(view, zr.at[i, p])
            sends.start(remote(view, view, zs.at[2, p], zr.at[2, p], to))
    pass_near(1)
    pass_near(3)
    acc[...] = jnp.zeros_like(acc)
    local.wait()
    add_shard(hd)
    arrived(ogv.at[2 * z + 1 - c], cr.at[0])
    add_shard(2 * z + 1 - c)
    pass_near(2)
    pass_pair(0)
    for i, s in ((0, below), (1, above)):
        for q in range(2):
            p = q + 2 - 2 * i
            arrived(ogv.at[s + c, quarter(p)], zr.at[i, p])
        sends.start(remote(ogv.at[s + c], ogv.at[s + c], cs.at[1 + i], cr.at[1 + i], other))
        add_shard(s + c)
    for i, s in ((0, below), (1, above)):
        arrived(ogv.at[s + 1 - c], cr.at[1 + i])
        add_shard(s + 1 - c)
    pass_pair(1)
    for p in range(4):
        arrived(ogv.at[across + c, quarter(p)], zr.at[2, p])
    sends.start(remote(ogv.at[across + c], ogv.at[across + c], cs.at[3], cr.at[3], other))
    add_shard(across + c)
    arrived(ogv.at[across + 1 - c], cr.at[3])
    add_shard(across + 1 - c)
    for k in range(HPD):
        dov[k] = acc[:, k * HD : (k + 1) * HD].astype(jnp.bfloat16)
    for dx in (2, 1, 3, 0):
        k = lax.rem(x + dx, SIDE)
        send_worker(dov.at[k], doa.at[rows_of(x)], ds.at[dx], dr.at[x], dx, k)
    pass_pair(3)
    pass_pair(2)
    for xs in range(SIDE):
        arrived(qa.at[rows_of(xs)], kr.at[xs, 2])
        arrived(doa.at[rows_of(xs)], dr.at[xs])
        for t, dst in ((0, ka), (1, va)):
            arrived(dst.at[rows_of(xs * SIDE + other_near)], fr.at[xs, t])
            arrived(dst.at[rows_of(xs * SIDE + other_pair_near)], fr.at[4 + xs, t])
    sends.wait()


UNROLL = 5


def attention_kernel(rid, rcnt, gid, q, do, k, v, o, dq, dk, dv, dka, dva, dkg, dvg):
    ctx, hd, x, y, z, c = place()
    ys = query_row(y, c)
    scale = 1.0 / math.sqrt(HD)
    f32, bf16 = jnp.float32, jnp.bfloat16
    dka[...] = jnp.zeros_like(dka)
    dva[...] = jnp.zeros_like(dva)
    dkg[...] = jnp.zeros_like(dkg)
    dvg[...] = jnp.zeros_like(dvg)

    def span(block, count):
        return pl.ds(pl.multiple_of(block * BLOCK, BLOCK), count * BLOCK)

    g0, g1 = span(gid[0], 1), span(gid[1], 1)
    column = lax.broadcasted_iota(jnp.int32, (1, 8 * BLOCK), 1) // BLOCK

    def listed(ref, window, randoms):
        return jnp.concatenate([ref[window, :], ref[g0, :], ref[g1, :]] + [ref[r, :] for r in randoms], axis=0)

    def step(m, carry):
        work = []
        for u in range(UNROLL):
            n = m * UNROLL + u
            xs = n // NBD
            i = (xs * SIDE + ys) * NBD + (n - xs * NBD)
            first = jnp.clip(i - 1, 0, NB - 3)
            window = span(first, 3)
            randoms = [span(rid[i * R + r], 1) for r in range(R)]
            low, high = i - 1 - first, i + 1 - first
            keep = ((column >= low) & (column <= high) & (column < 3)) | (
                (column >= 3) & (column < 5 + rcnt[i])
            )
            bias = jnp.where(keep, 0.0, -1e30).astype(f32)
            work.append((span(n, 1), window, randoms, bias))
        kc = [listed(k, window, randoms) for _, window, randoms, _ in work]
        vc = [listed(v, window, randoms) for _, window, randoms, _ in work]
        qn = [q[mine, :] for mine, _, _, _ in work]
        dn = [do[mine, :] for mine, _, _, _ in work]
        s = [
            lax.dot_general(a, b, NT, preferred_element_type=f32) * scale + t[3]
            for a, b, t in zip(qn, kc, work)
        ]
        dp = [lax.dot_general(a, b, NT, preferred_element_type=f32) for a, b in zip(dn, vc)]
        e = [jnp.exp(a - jnp.max(a, axis=1, keepdims=True)) for a in s]
        p = [a * (1.0 / jnp.sum(a, axis=1, keepdims=True)) for a in e]
        low_p = [a.astype(bf16) for a in p]
        on = [jnp.dot(a, b, preferred_element_type=f32).astype(bf16) for a, b in zip(low_p, vc)]
        delta = [
            jnp.sum(a.astype(f32) * b.astype(f32), axis=1, keepdims=True) for a, b in zip(dn, on)
        ]
        dsc = [(a * (b - d)).astype(bf16) for a, b, d in zip(p, dp, delta)]
        dvt = [lax.dot_general(a, b, TN, preferred_element_type=f32) for a, b in zip(low_p, dn)]
        dkt = [lax.dot_general(a, b, TN, preferred_element_type=f32) for a, b in zip(dsc, qn)]
        dqn = [
            (jnp.dot(a, b, preferred_element_type=f32) * scale).astype(bf16) for a, b in zip(dsc, kc)
        ]
        for t, a, b in zip(work, on, dqn):
            o[t[0], :] = a
            dq[t[0], :] = b
        for total, glob, terms in ((dka, dkg, dkt), (dva, dvg, dvt)):
            glob[...] += sum(a[3 * BLOCK : 5 * BLOCK] for a in terms)
            for (_, window, randoms, _), a in zip(work, terms):
                total[window, :] += a[: 3 * BLOCK]
                for r in range(R):
                    total[randoms[r], :] += a[(5 + r) * BLOCK : (6 + r) * BLOCK]
        return carry

    lax.fori_loop(0, 4 * NBD // UNROLL, step, 0)
    for total, glob in ((dka, dkg), (dva, dvg)):
        total[g0, :] += glob[:BLOCK]
        total[g1, :] += glob[BLOCK:]

    def finish(n, carry):
        part = pl.ds(pl.multiple_of(n * 256, 256), 256)
        dk[part, :] = (dka[part, :] * scale).astype(bf16)
        dv[part, :] = dva[part, :].astype(bf16)
        return carry

    lax.fori_loop(0, NB * BLOCK // 256, finish, 0)


def return_kernel(
    oa, dqa, dka, dva, w, proj, dqh, dkh, dvh,
    oh, part_out, core_in, hop_in, z_in, held, dmine, dcore, dpair,
    os, orr, qs, qr, es, er, ls, ps, pr, hs, hr, cs, cr, as_, ar, zs, zr,
):
    ctx, hd, x, y, z, c = place()
    f32, bf16 = jnp.float32, jnp.bfloat16
    half = y // 2
    pair, other, up, down = neighbours(x, y, z, c)
    cw = lax.rem(half + c, 2)
    yw = query_row(y, cw)
    py = y + 1 - 2 * lax.rem(y, 2)
    near, pair_near = query_row(y, c), query_row(py, c)
    other_near, other_pair_near = query_row(y, 1 - c), query_row(py, 1 - c)
    to_self = 1 - jnp.minimum(c + half, 1)
    me = to_self == 1

    senders = [
        ({"ctx": lax.rem(x + dx, SIDE) * SIDE + yw, "head": 2 * z + cw}, None if dx else me)
        for dx in range(SIDE)
    ]
    enter(senders + [(up, None), (down, None), (other, None), (pair, None)], to_self)

    sends = Sends()

    def send_home(src, dst, send, recv, dx):
        home = {"ctx": lax.rem(x + dx, SIDE) * SIDE + near, "head": 2 * z + half}
        if dx:
            sends.start(remote(src, dst, send, recv, home))
        else:
            sends.start_unless(me, src, dst, send, recv, home)

    def arrived(view, recv):
        remote(view, view, recv, recv, other).wait_recv()

    for dx in (2, 1, 3, 0):
        send_home(oa.at[rows_of(lax.rem(x + dx, SIDE))], oh.at[x], os.at[dx], orr.at[x], dx)
    for g, there, here in ((0, other_pair_near, pair_near), (4, other_near, near)):
        for dx in (2, 1, 3, 0):
            xs = lax.rem(x + dx, SIDE)
            for t, src in ((0, dka), (1, dva)):
                j = g + xs
                sends.start(
                    remote(src.at[rows_of(xs * SIDE + there)], dcore.at[j, t], es.at[j, t], er.at[j, t], other)
                )
                pltpu.make_async_copy(
                    src.at[rows_of(xs * SIDE + here)], dmine.at[j, t], ls.at[j, t]
                ).start()
    for dx in (2, 1, 3, 0):
        send_home(dqa.at[rows_of(lax.rem(x + dx, SIDE))], dqh.at[x], qs.at[dx], qr.at[x], dx)

    def cores_met(j, t):
        pltpu.make_async_copy(dmine.at[j, t], dmine.at[j, t], ls.at[j, t]).wait()
        arrived(dcore.at[j, t], er.at[j, t])

    for dx in (2, 1, 3, 0):
        xs = lax.rem(x + dx, SIDE)
        for t in range(2):
            cores_met(xs, t)
            dmine[xs, t] = (dmine[xs, t].astype(f32) + dcore[xs, t].astype(f32)).astype(bf16)
            sends.start(remote(dmine.at[xs, t], dpair.at[xs, t], ps.at[xs, t], pr.at[xs, t], pair))

    def finish(dx):
        xs = lax.rem(x + dx, SIDE)
        for t, out in ((0, dkh), (1, dvh)):
            cores_met(4 + xs, t)
            arrived(dpair.at[xs, t], pr.at[xs, t])
            dmine[4 + xs, t] = (
                dmine[4 + xs, t].astype(f32) + dcore[4 + xs, t].astype(f32) + dpair[xs, t].astype(f32)
            ).astype(bf16)
            send_home(dmine.at[4 + xs, t], out.at[x], hs.at[dx, t], hr.at[x, t], dx)

    for k in range(HPD):
        arrived(oh.at[k], orr.at[k])

    def shard_product(s, put):
        columns = pl.ds(pl.multiple_of(s * SHARD, SHARD), SHARD)

        def tile(i, carry):
            part = pl.ds(pl.multiple_of(i * QUARTER, QUARTER), QUARTER)
            rows = jnp.concatenate([oh[k, part, :] for k in range(HPD)], axis=1)
            put(part, jnp.dot(rows, w[:, columns], preferred_element_type=f32))
            return carry

        lax.fori_loop(0, 4, tile, 0)

    below = 2 * lax.rem(z + 3, SIDE)
    above = 2 * lax.rem(z + 1, SIDE)
    across = 2 * lax.rem(z + 2, SIDE)

    for i, s in enumerate((across, above, below, 2 * z)):

        def put(part, value):
            part_out[i, part, :] = value.astype(bf16)

        shard_product(s + 1 - c, put)
        sends.start(remote(part_out.at[i], core_in.at[i], cs.at[i], cr.at[i], other))

    arrived(core_in.at[0], cr.at[0])

    def put_across(part, value):
        part_out[4, part, :] = (value + core_in[0, part, :].astype(f32)).astype(bf16)

    shard_product(across + c, put_across)
    for q in range(4):
        sends.start(
            remote(
                part_out.at[4, quarter(q)], hop_in.at[quarter(q)], as_.at[q], ar.at[q], up if q < 2 else down
            )
        )
    for i, s, to in ((0, above, up), (1, below, down)):
        arrived(core_in.at[1 + i], cr.at[1 + i])

        def put_near(part, value):
            part_out[5 + i, part, :] = (value + core_in[1 + i, part, :].astype(f32)).astype(bf16)

        shard_product(s + c, put_near)
        for q in (2 - 2 * i, 3 - 2 * i):
            sends.start(
                remote(part_out.at[5 + i, quarter(q)], z_in.at[i, quarter(q)], zs.at[i, q], zr.at[i, q], to)
            )
    arrived(core_in.at[3], cr.at[3])

    def put_own(part, value):
        held[part, :] = value + core_in[3, part, :].astype(f32)

    shard_product(hd, put_own)
    finish(2)
    for q in range(2):
        for i, to in ((0, up), (1, down)):
            p = q + 2 * i
            arrived(hop_in.at[quarter(p)], ar.at[p])
            part_out[5 + i, quarter(p), :] = (
                part_out[5 + i, quarter(p), :].astype(f32) + hop_in[quarter(p), :].astype(f32)
            ).astype(bf16)
            sends.start(
                remote(part_out.at[5 + i, quarter(p)], z_in.at[i, quarter(p)], zs.at[i, p], zr.at[i, p], to)
            )
    for dx in (1, 3, 0):
        finish(dx)
    for i in range(2):
        for q in range(4):
            arrived(z_in.at[i, quarter(q)], zr.at[i, q])
    proj[...] = (held[...] + z_in[0].astype(f32) + z_in[1].astype(f32)).astype(bf16)
    for k in range(HPD):
        arrived(dqh.at[k], qr.at[k])
        arrived(dkh.at[k], hr.at[k, 0])
        arrived(dvh.at[k], hr.at[k, 1])
    sends.wait()


ANY = pl.BlockSpec(memory_space=pl.ANY)
VMEM = pl.BlockSpec(memory_space=pltpu.VMEM)
SMEM = pl.BlockSpec(memory_space=pltpu.SMEM)
LIMIT = 56 * 1024 * 1024


def struct(*shape):
    return jax.ShapeDtypeStruct(shape, jnp.bfloat16)


def sem(*shape):
    return pltpu.SemaphoreType.DMA(shape)


def local(queries, key_rows, value_rows, out_weight, out_grad, global_ids, random_ids, random_count):
    bf16, f32 = jnp.bfloat16, jnp.float32
    kvq = jnp.transpose(jnp.stack([key_rows, value_rows, queries], axis=0), (2, 0, 1, 3))
    w = out_weight.reshape(HPD * HD, out_weight.shape[2])
    tokens = NB * BLOCK
    ka, va, qa, doa = pl.pallas_call(
        gather_kernel,
        out_shape=(struct(tokens, HD), struct(tokens, HD), struct(4 * HERE, HD), struct(4 * HERE, HD)),
        in_specs=[ANY, ANY, VMEM],
        out_specs=(ANY,) * 4,
        scratch_shapes=[
            pltpu.VMEM((8, HERE, SHARD), bf16),
            pltpu.VMEM((HERE, SHARD), f32),
            pltpu.VMEM((HPD, HERE, HD), bf16),
            sem(4, 3), sem(4, 3), sem(4, 2), sem(4, 2), sem(8, 2), sem(8, 2), sem(4), sem(4),
            sem(3, 4), sem(3, 4), sem(4), sem(4), pltpu.SemaphoreType.DMA,
        ],
        compiler_params=pltpu.CompilerParams(
            collective_id=0, has_side_effects=True, vmem_limit_bytes=LIMIT
        ),
    )(kvq, out_grad, w)
    oa, dqa, dka, dva = pl.pallas_call(
        attention_kernel,
        out_shape=(struct(4 * HERE, HD), struct(4 * HERE, HD), struct(tokens, HD), struct(tokens, HD)),
        in_specs=[SMEM] * 3 + [VMEM] * 4,
        out_specs=(VMEM,) * 4,
        scratch_shapes=[
            pltpu.VMEM((tokens, HD), f32),
            pltpu.VMEM((tokens, HD), f32),
            pltpu.VMEM((2 * BLOCK, HD), f32),
            pltpu.VMEM((2 * BLOCK, HD), f32),
        ],
        compiler_params=pltpu.CompilerParams(vmem_limit_bytes=LIMIT),
    )(random_ids.reshape(NB * R), random_count, global_ids, qa, doa, ka, va)
    projected, dqh, dkh, dvh = pl.pallas_call(
        return_kernel,
        out_shape=(struct(HERE, SHARD),) + (struct(HPD, HERE, HD),) * 3,
        in_specs=[ANY] * 4 + [VMEM],
        out_specs=(VMEM, ANY, ANY, ANY),
        scratch_shapes=[
            pltpu.VMEM((HPD, HERE, HD), bf16),
            pltpu.VMEM((7, HERE, SHARD), bf16),
            pltpu.VMEM((4, HERE, SHARD), bf16),
            pltpu.VMEM((HERE, SHARD), bf16),
            pltpu.VMEM((2, HERE, SHARD), bf16),
            pltpu.VMEM((HERE, SHARD), f32),
            pltpu.VMEM((8, 2, HERE, HD), bf16),
            pltpu.VMEM((8, 2, HERE, HD), bf16),
            pltpu.VMEM((4, 2, HERE, HD), bf16),
            sem(4), sem(4), sem(4), sem(4), sem(8, 2), sem(8, 2), sem(8, 2), sem(4, 2), sem(4, 2),
            sem(4, 2), sem(4, 2), sem(4), sem(4), sem(4), sem(4), sem(2, 4), sem(2, 4),
        ],
        compiler_params=pltpu.CompilerParams(
            collective_id=1, has_side_effects=True, vmem_limit_bytes=LIMIT
        ),
    )(oa, dqa, dka, dva, w)
    grads = [jnp.transpose(g, (1, 0, 2)) for g in (dqh, dkh, dvh)]
    return (projected, *grads)


def solution(mesh):
    placed = (
        P("ctx", "head", None),
        P("ctx", "head", None),
        P("ctx", "head", None),
        P("head", None, None),
        P("ctx", "head"),
        P(),
        P(),
        P(),
    )
    return jax.shard_map(
        local,
        mesh=mesh,
        in_specs=placed,
        out_specs=(
            P("ctx", "head"),
            P("ctx", "head", None),
            P("ctx", "head", None),
            P("ctx", "head", None),
        ),
        check_vma=False,
    )
```

```python
import functools
import math

import jax
import jax.numpy as jnp
from jax import lax
from jax.experimental import pallas as pl
from jax.experimental.pallas import tpu as pltpu
from jax.sharding import PartitionSpec as P

SIDE = 4
BLOCK = 64
G = 2
R = 3
HERE = 640
NBD = 10
HD = 128
HPD = 4
NB = 160
SHARD = 512
MESH = pl.DeviceIdType.MESH
NT = (((1,), (1,)), ((), ()))
TN = (((0,), (0,)), ((), ()))


def place():
    ctx, hd = lax.axis_index("ctx"), lax.axis_index("head")
    return ctx, hd, ctx // SIDE, lax.rem(ctx, SIDE), hd // 2, lax.rem(hd, 2)


def query_row(y, c):
    return y * (1 - c) + (3 - y) * c


def remote(src, dst, send, recv, device):
    return pltpu.make_async_remote_copy(
        src_ref=src, dst_ref=dst, send_sem=send, recv_sem=recv, device_id=device, device_id_type=MESH
    )


def greet(device):
    pl.semaphore_signal(pltpu.get_barrier_semaphore(), inc=1, device_id=device, device_id_type=MESH)


def blocks_of(index):
    return pl.ds(index * NBD, NBD)


PIECES = 2
PIECE = HERE // PIECES
CUT = NBD // PIECES


def padded(index, h):
    return pl.ds(1 + index * NBD + h * CUT, CUT)


def pieces(*refs):
    return [(t * PIECES + h, h, t, ref) for h in range(PIECES) for t, ref in enumerate(refs)]


def neighbours(x, y, z, c):
    pair = {"ctx": x * SIDE + y + 1 - 2 * lax.rem(y, 2)}
    other = {"head": 2 * z + 1 - c}
    up = {"head": 2 * lax.rem(z + 1, SIDE) + c}
    down = {"head": 2 * lax.rem(z + 3, SIDE) + c}
    return pair, other, up, down


def enter(senders, to_self):
    for device, mine in senders:
        if mine is None:
            greet(device)
        else:
            pl.when(jnp.logical_not(mine))(functools.partial(greet, device))
    pl.semaphore_wait(pltpu.get_barrier_semaphore(), len(senders) - to_self)


class Sends:
    def __init__(self):
        self.started, self.guarded = [], []

    def start(self, copy):
        copy.start()
        self.started.append(copy)

    def start_unless(self, mine, src, dst, send, recv, device):
        copy = remote(src, dst, send, recv, device)
        here = pltpu.make_async_copy(src, dst, recv)
        pl.when(jnp.logical_not(mine))(copy.start)
        pl.when(mine)(here.start)
        self.guarded.append((copy, mine))

    def wait(self):
        for copy in self.started:
            copy.wait_send()
        for copy, mine in self.guarded:
            pl.when(jnp.logical_not(mine))(copy.wait_send)


QUARTER = HERE // 4


def quarter(q):
    return pl.ds(q * QUARTER, QUARTER)


UNROLL = 5
MASKED = -1e30
NR = 4 * NBD * R
LAST = NR + G
LISTED = LAST + NB


def layer_kernel(
    aux, off, kvq, og, w, proj, dqh, dkh, dvh,
    ka, va, qa, doa, oa, dqa, ogv, acc, dov, wv, dka, dva, dkg, dvg, runk, runv,
    oh, core_in, hop_in, z_in, stage, dcore, psend, nsend, dpair,
    ks, kr, qs, qr, ps, pr, fs, fr, ds, dr, zs, zr, cs, cr, own, wsem,
    os, orr, gs, gr, es, er, bs, br, hs, hr, c2s, c2r, as_, ar, z2s, z2r,
):
    ctx, hd, x, y, z, c = place()
    f32, bf16 = jnp.float32, jnp.bfloat16
    half = y // 2
    pair, other, up, down = neighbours(x, y, z, c)
    cw = lax.rem(half + c, 2)
    yw = query_row(y, cw)
    py = y + 1 - 2 * lax.rem(y, 2)
    near, pair_near = query_row(y, c), query_row(py, c)
    other_near, other_pair_near = query_row(y, 1 - c), query_row(py, 1 - c)
    to_self = 1 - jnp.minimum(c + half, 1)
    me = to_self == 1

    def worker(k):
        return {"ctx": k * SIDE + yw, "head": 2 * z + cw}

    senders = [
        ({"ctx": lax.rem(x + dx, SIDE) * SIDE + near, "head": 2 * z + half}, None if dx else me)
        for dx in range(SIDE)
    ]
    local = pltpu.make_async_copy(og, ogv.at[hd], own)
    local.start()
    weight = pltpu.make_async_copy(w, wv, wsem)
    weight.start()
    receivers = [
        ({"ctx": lax.rem(x + dx, SIDE) * SIDE + yw, "head": 2 * z + cw}, None if dx else me)
        for dx in range(SIDE)
    ]
    enter(senders + receivers + [(up, None), (down, None), (other, None), (pair, None)], 2 * to_self)

    sends, early = Sends(), Sends()

    def send_worker(src, dst, send, recv, dx, k):
        if dx:
            sends.start(remote(src, dst, send, recv, worker(k)))
        else:
            sends.start_unless(me, src, dst, send, recv, worker(k))

    def arrived(view, recv):
        remote(view, view, recv, recv, other).wait_recv()

    def send_pieces(dxs):
        for m, h, t, dst in pieces(ka, va):
            for dx in dxs:
                k = lax.rem(x + dx, SIDE)
                src = kvq.at[k, t, pl.ds(h * CUT, CUT)]
                send_worker(src, dst.at[padded(ctx, h)], ks.at[dx, m], kr.at[x, m], dx, k)

    send_pieces((0,))
    for q in range(4):
        for i, to, p in ((0, up, q), (1, down, (q + 2) % 4)):
            sends.start(remote(og.at[quarter(p)], ogv.at[hd, quarter(p)], zs.at[i, p], zr.at[i, p], to))
    send_pieces((1, 3))
    sends.start(remote(og, ogv.at[hd], cs.at[0], cr.at[0], other))
    dka[...] = jnp.zeros_like(dka)
    dva[...] = jnp.zeros_like(dva)
    for ref in (dkg, dvg):
        ref[...] = jnp.zeros_like(ref)
    for ref in (ka, va):
        ref[0] = jnp.zeros((BLOCK, HD), bf16)
        ref[NB + 1] = jnp.zeros((BLOCK, HD), bf16)
    for ref in (runk, runv):
        ref[0] = jnp.zeros((BLOCK, HD), f32)

    def add_shard(s):
        columns = pl.ds(pl.multiple_of(s * SHARD, SHARD), SHARD)

        def tile(i, carry):
            part = pl.ds(pl.multiple_of(i * PIECE, PIECE), PIECE)
            acc[part, :] += lax.dot_general(
                ogv[s, part, :], wv[:, columns], NT, preferred_element_type=f32
            )
            return carry

        lax.fori_loop(0, PIECES, tile, 0)

    def pass_near(dxs):
        for m, h, t, dst in pieces(ka, va):
            for dx in dxs:
                xs = lax.rem(x + SIDE - dx, SIDE)
                view = dst.at[padded(xs * SIDE + near, h)]
                arrived(view, kr.at[xs, m])
                sends.start(remote(view, view, ps.at[xs, m], pr.at[xs, m], pair))
                sends.start(remote(view, view, fs.at[xs, m], fr.at[xs, m], other))

    def pass_pair(dx):
        xs = lax.rem(x + SIDE - dx, SIDE)
        for m, h, t, dst in pieces(ka, va):
            view = dst.at[padded(xs * SIDE + pair_near, h)]
            arrived(view, pr.at[xs, m])
            sends.start(remote(view, view, fs.at[4 + xs, m], fr.at[4 + xs, m], other))

    below = 2 * lax.rem(z + 3, SIDE)
    above = 2 * lax.rem(z + 1, SIDE)
    across = 2 * lax.rem(z + 2, SIDE)

    pass_near((0,))
    for q in range(2):
        for i, s, to, p in ((0, below, up, q), (1, above, down, q + 2)):
            view = ogv.at[s + c, quarter(p)]
            arrived(view, zr.at[i, p])
            early.start(remote(view, view, zs.at[2, p], zr.at[2, p], to))
    pass_near((1, 3))
    send_pieces((2,))
    for dx in (0, 1, 3, 2):
        k = lax.rem(x + dx, SIDE)
        send_worker(kvq.at[k, 2], qa.at[blocks_of(x)], qs.at[dx], qr.at[x], dx, k)
    acc[...] = jnp.zeros_like(acc)
    local.wait()
    weight.wait()
    add_shard(hd)
    arrived(ogv.at[2 * z + 1 - c], cr.at[0])
    add_shard(2 * z + 1 - c)
    pass_near((2,))
    pass_pair(0)
    for i, s in ((0, below), (1, above)):
        for q in range(2):
            p = q + 2 - 2 * i
            arrived(ogv.at[s + c, quarter(p)], zr.at[i, p])
        early.start(remote(ogv.at[s + c], ogv.at[s + c], cs.at[1 + i], cr.at[1 + i], other))
        add_shard(s + c)
    for i, s in ((0, below), (1, above)):
        arrived(ogv.at[s + 1 - c], cr.at[1 + i])
        add_shard(s + 1 - c)
    pass_pair(1)
    for p in range(4):
        arrived(ogv.at[across + c, quarter(p)], zr.at[2, p])
    early.start(remote(ogv.at[across + c], ogv.at[across + c], cs.at[3], cr.at[3], other))
    add_shard(across + c)
    arrived(ogv.at[across + 1 - c], cr.at[3])
    add_shard(across + 1 - c)
    for k in range(HPD):
        dov[k] = acc[:, k * HD : (k + 1) * HD].astype(bf16).reshape(NBD, BLOCK, HD)
    for dx in (2, 1, 3, 0):
        k = lax.rem(x + dx, SIDE)
        send_worker(dov.at[k], doa.at[blocks_of(x)], ds.at[dx], dr.at[x], dx, k)
    pass_pair(3)
    pass_pair(2)
    for xs in range(SIDE):
        arrived(qa.at[blocks_of(xs)], qr.at[xs])
        arrived(doa.at[blocks_of(xs)], dr.at[xs])
        for m, h, t, dst in pieces(ka, va):
            arrived(dst.at[padded(xs * SIDE + other_near, h)], fr.at[xs, m])
            arrived(dst.at[padded(xs * SIDE + other_pair_near, h)], fr.at[4 + xs, m])

    scale = 1.0 / math.sqrt(HD)

    def named(entry):
        return aux[LISTED + entry]

    g0, g1 = named(NR), named(NR + 1)
    column = lax.broadcasted_iota(jnp.int32, (1, 8 * BLOCK), 1) // BLOCK
    entry_is = [jnp.where(column == j, 1.0, 0.0).astype(f32) for j in range(8)]

    def listed(ref, window, randoms):
        near_rows = ref[window].reshape(3 * BLOCK, HD)
        return jnp.concatenate([near_rows, ref[g0], ref[g1]] + [ref[r] for r in randoms], axis=0)

    def step(turn, xs, m):
        work = []
        for u in range(UNROLL):
            block = m * UNROLL + u
            n = turn * NBD + block
            i = (xs * SIDE + near) * NBD + block
            bias = entry_is[0] * jnp.where(i == 0, MASKED, 0.0) + entry_is[2] * jnp.where(i == NB - 1, MASKED, 0.0)
            for r in range(R):
                bias = bias + entry_is[5 + r] * off[n * R + r]
            randoms = [named(n * R + r) for r in range(R)]
            work.append((xs * NBD + block, pl.ds(i, 3), randoms, bias, n))
        kc = [listed(ka, t[1], t[2]) for t in work]
        vc = [listed(va, t[1], t[2]) for t in work]
        qn = [qa[t[0]] for t in work]
        dn = [doa[t[0]] for t in work]
        s = [
            lax.dot_general(a, b, NT, preferred_element_type=f32) * scale + t[3]
            for a, b, t in zip(qn, kc, work)
        ]
        dp = [lax.dot_general(a, b, NT, preferred_element_type=f32) for a, b in zip(dn, vc)]
        e = [jnp.exp(a - jnp.max(a, axis=1, keepdims=True)) for a in s]
        p = [a * (1.0 / jnp.sum(a, axis=1, keepdims=True)) for a in e]
        low_p = [a.astype(bf16) for a in p]
        on = [jnp.dot(a, b, preferred_element_type=f32).astype(bf16) for a, b in zip(low_p, vc)]
        delta = [
            jnp.sum(a.astype(f32) * b.astype(f32), axis=1, keepdims=True) for a, b in zip(dn, on)
        ]
        dsc = [(a * (b - d)).astype(bf16) for a, b, d in zip(p, dp, delta)]
        dvt = [lax.dot_general(a, b, TN, preferred_element_type=f32) for a, b in zip(low_p, dn)]
        dkt = [lax.dot_general(a, b, TN, preferred_element_type=f32) for a, b in zip(dsc, qn)]
        dqn = [
            (jnp.dot(a, b, preferred_element_type=f32) * scale).astype(bf16) for a, b in zip(dsc, kc)
        ]
        for t, a, b in zip(work, on, dqn):
            oa[t[0]] = a
            dqa[t[0]] = b
        for total, glob, run, terms in ((dka, dkg, runk, dkt), (dva, dvg, runv, dvt)):
            glob[...] += sum(a[3 * BLOCK : 5 * BLOCK] for a in terms).reshape(G, BLOCK, HD)
            for t, a in zip(work, terms):
                total[t[1]] += a[: 3 * BLOCK].reshape(3, BLOCK, HD)
                for r in range(R):
                    entry = t[4] * R + r
                    run[entry + 1] = a[(5 + r) * BLOCK : (6 + r) * BLOCK] + run[aux[entry]]

    def home_of(xs):
        return {"ctx": xs * SIDE + near, "head": 2 * z + half}

    def source_turn(turn, carry):
        xs = lax.rem(x + turn + 1, SIDE)

        def half_turn(m, inner):
            step(turn, xs, m)
            return inner

        lax.fori_loop(0, NBD // UNROLL, half_turn, 0)
        mine = me & (turn == SIDE - 1)
        for src, dst, send, recv in ((oa, oh, os, orr), (dqa, dqh, gs, gr)):
            copy = remote(src.at[blocks_of(xs)], dst.at[x], send.at[turn], recv.at[x], home_of(xs))
            here = pltpu.make_async_copy(src.at[blocks_of(xs)], dst.at[x], recv.at[x])
            pl.when(jnp.logical_not(mine))(copy.start)
            pl.when(mine)(here.start)
        return carry

    lax.fori_loop(0, SIDE, source_turn, 0)
    for i in range(SIDE):
        xs = lax.rem(x + i + 1, SIDE)
        for src, dst, send, recv in ((oa, oh, os, orr), (dqa, dqh, gs, gr)):
            copy = remote(src.at[blocks_of(xs)], dst.at[x], send.at[i], recv.at[x], home_of(xs))
            if i < SIDE - 1:
                sends.started.append(copy)
            else:
                sends.guarded.append((copy, me))
    for run, glob in ((runk, dkg), (runv, dvg)):
        for i in range(G):
            run[NR + i + 1] = glob[i] + run[aux[NR + i]]
    early.wait()

    def put_sum(ref, j, t, h, total, run, index, factor, also):
        def block(n, carry):
            here = h * CUT + n
            u = index * NBD + here
            value = (total[u + 1] + run[aux[LAST + u]]) * factor
            for other_ref, slot in also:
                value = value + other_ref[slot, t, here].astype(f32)
            ref[j, t, here] = value.astype(bf16)
            return carry

        lax.fori_loop(0, CUT, block, 0)

    totals = ((dka, runk, scale), (dva, runv, 1.0))

    def part(h):
        return pl.ds(h * CUT, CUT)

    def for_other_core(g, there, dx):
        xs = lax.rem(x + dx, SIDE)
        for m, h, t, (total, run, factor) in pieces(*totals):
            put_sum(stage, g + xs, t, h, total, run, xs * SIDE + there, factor, ())
            sends.start(
                remote(stage.at[g + xs, t, part(h)], dcore.at[g + xs, t, part(h)], es.at[g + xs, m], er.at[g + xs, m], other)
            )

    def for_pair(dx):
        xs = lax.rem(x + dx, SIDE)
        for m, h, t, (total, run, factor) in pieces(*totals):
            arrived(dcore.at[xs, t, part(h)], er.at[xs, m])
            put_sum(psend, xs, t, h, total, run, xs * SIDE + pair_near, factor, ((dcore, xs),))
            sends.start(
                remote(psend.at[xs, t, part(h)], dpair.at[xs, t, part(h)], bs.at[xs, m], br.at[xs, m], pair)
            )

    def finish(dx):
        xs = lax.rem(x + dx, SIDE)
        for m, h, t, (total, run, factor) in pieces(*totals):
            arrived(dcore.at[4 + xs, t, part(h)], er.at[4 + xs, m])
            arrived(dpair.at[xs, t, part(h)], br.at[xs, m])
            put_sum(
                nsend, xs, t, h, total, run, xs * SIDE + near, factor, ((dcore, 4 + xs), (dpair, xs))
            )
            src, dst = nsend.at[xs, t, part(h)], (dkh, dvh)[t].at[x, part(h)]
            if dx:
                sends.start(remote(src, dst, hs.at[dx, m], hr.at[x, m], home_of(xs)))
            else:
                sends.start_unless(me, src, dst, hs.at[dx, m], hr.at[x, m], home_of(xs))

    for dx in (2, 1, 3, 0):
        for_other_core(0, other_pair_near, dx)
    for_pair(2)
    for_pair(1)
    for k in range(HPD):
        arrived(oh.at[k], orr.at[k])

    def shard_product(s, put):
        columns = pl.ds(pl.multiple_of(s * SHARD, SHARD), SHARD)

        def tile(i, carry):
            rows = pl.ds(pl.multiple_of(i * PIECE, PIECE), PIECE)
            left = [oh[k, pl.ds(i * CUT, CUT)].reshape(PIECE, HD) for k in range(HPD)]
            left = jnp.concatenate(left, axis=1)
            put(rows, jnp.dot(left, wv[:, columns], preferred_element_type=f32))
            return carry

        lax.fori_loop(0, PIECES, tile, 0)

    for i, s in enumerate((across, above, below, 2 * z)):

        def put(rows, value):
            ogv[i, rows, :] = value.astype(bf16)

        shard_product(s + 1 - c, put)
        sends.start(remote(ogv.at[i], core_in.at[i], c2s.at[i], c2r.at[i], other))

    arrived(core_in.at[0], c2r.at[0])

    def put_across(rows, value):
        ogv[4, rows, :] = (value + core_in[0, rows, :].astype(f32)).astype(bf16)

    shard_product(across + c, put_across)
    for q in range(4):
        sends.start(
            remote(
                ogv.at[4, quarter(q)], hop_in.at[quarter(q)], as_.at[q], ar.at[q], up if q < 2 else down
            )
        )
    for i, s, to in ((0, above, up), (1, below, down)):
        arrived(core_in.at[1 + i], c2r.at[1 + i])

        def put_near(rows, value):
            ogv[5 + i, rows, :] = (value + core_in[1 + i, rows, :].astype(f32)).astype(bf16)

        shard_product(s + c, put_near)
        for q in (2 - 2 * i, 3 - 2 * i):
            sends.start(
                remote(ogv.at[5 + i, quarter(q)], z_in.at[i, quarter(q)], z2s.at[i, q], z2r.at[i, q], to)
            )
    arrived(core_in.at[3], c2r.at[3])

    def put_own(rows, value):
        acc[rows, :] = value + core_in[3, rows, :].astype(f32)

    for_pair(3)
    for_pair(0)
    for dx in (2, 1, 3, 0):
        for_other_core(4, other_near, dx)
    shard_product(hd, put_own)
    for q in range(2):
        for i, to in ((0, up), (1, down)):
            p = q + 2 * i
            arrived(hop_in.at[quarter(p)], ar.at[p])
            ogv[5 + i, quarter(p), :] = (
                ogv[5 + i, quarter(p), :].astype(f32) + hop_in[quarter(p), :].astype(f32)
            ).astype(bf16)
            sends.start(
                remote(ogv.at[5 + i, quarter(p)], z_in.at[i, quarter(p)], z2s.at[i, p], z2r.at[i, p], to)
            )
    for dx in (2, 1, 3, 0):
        finish(dx)
    for i in range(2):
        for q in range(4):
            arrived(z_in.at[i, quarter(q)], z2r.at[i, q])
    proj[...] = (acc[...] + z_in[0].astype(f32) + z_in[1].astype(f32)).astype(bf16)
    for k in range(HPD):
        arrived(dqh.at[k], gr.at[k])
        for m, h, t, out in pieces(dkh, dvh):
            arrived(out.at[k, part(h)], hr.at[k, m])
    sends.wait()


ANY = pl.BlockSpec(memory_space=pl.ANY)
VMEM = pl.BlockSpec(memory_space=pltpu.VMEM)
SMEM = pl.BlockSpec(memory_space=pltpu.SMEM)
LIMIT = 60 * 1024 * 1024


def struct(*shape):
    return jax.ShapeDtypeStruct(shape, jnp.bfloat16)


def sem(*shape):
    return pltpu.SemaphoreType.DMA(shape)


def entries(global_ids, random_ids, random_count):
    _, _, x, y, _, c = place()
    near = query_row(y, c)

    def mine(table):
        rows = lax.dynamic_index_in_dim(table.reshape(SIDE, SIDE, -1), near, 1, keepdims=False)
        return lax.dynamic_slice_in_dim(jnp.concatenate([rows, rows], axis=0), x + 1, SIDE, 0).reshape(-1)

    listed = jnp.concatenate([mine(random_ids), global_ids])
    number = jnp.arange(NR + G, dtype=jnp.int32)
    wanted = jnp.concatenate([listed, jnp.arange(NB, dtype=jnp.int32)])
    limit = jnp.concatenate([number, jnp.full((NB,), NR + G, jnp.int32)])
    hit = (listed[None, :] == wanted[:, None]) & (number[None, :] < limit[:, None])
    chain = jnp.max(jnp.where(hit, number[None, :] + 1, 0), axis=1)
    valid = jnp.arange(R, dtype=jnp.int32)[None, :] < mine(random_count)[:, None]
    return jnp.concatenate([chain, listed + 1]), jnp.where(valid, 0.0, MASKED).astype(jnp.float32).reshape(-1)


def local(queries, key_rows, value_rows, out_weight, out_grad, global_ids, random_ids, random_count):
    bf16, f32 = jnp.bfloat16, jnp.float32
    kvq = jnp.transpose(jnp.stack([key_rows, value_rows, queries], axis=0), (2, 0, 1, 3))
    kvq = kvq.reshape(HPD, 3, NBD, BLOCK, HD)
    w = out_weight.reshape(HPD * HD, out_weight.shape[2])
    both = 2 * PIECES

    def vmem(*shape, dtype=bf16):
        return pltpu.VMEM(shape, dtype)

    def blocks(*count, dtype=bf16):
        return vmem(*count, BLOCK, HD, dtype=dtype)

    one = pltpu.SemaphoreType.DMA
    projected, dqh, dkh, dvh = pl.pallas_call(
        layer_kernel,
        out_shape=(struct(HERE, SHARD),) + (struct(HPD, NBD, BLOCK, HD),) * 3,
        in_specs=[SMEM, SMEM, ANY, ANY, ANY],
        out_specs=(VMEM, ANY, ANY, ANY),
        scratch_shapes=[
            blocks(NB + 2), blocks(NB + 2), blocks(4 * NBD), blocks(4 * NBD), blocks(4 * NBD), blocks(4 * NBD),
            vmem(8, HERE, SHARD), vmem(HERE, SHARD, dtype=f32), blocks(HPD, NBD), vmem(*w.shape),
            blocks(NB + 2, dtype=f32), blocks(NB + 2, dtype=f32), blocks(G, dtype=f32), blocks(G, dtype=f32),
            blocks(NR + G + 1, dtype=f32), blocks(NR + G + 1, dtype=f32),
            blocks(HPD, NBD), vmem(4, HERE, SHARD), vmem(HERE, SHARD), vmem(2, HERE, SHARD),
            blocks(8, 2, NBD), blocks(8, 2, NBD), blocks(4, 2, NBD), blocks(4, 2, NBD), blocks(4, 2, NBD),
            sem(4, both), sem(4, both), sem(4), sem(4), sem(4, both), sem(4, both), sem(8, both), sem(8, both),
            sem(4), sem(4), sem(3, 4), sem(3, 4), sem(4), sem(4), one, one,
            sem(4), sem(4), sem(4), sem(4), sem(8, both), sem(8, both), sem(4, both), sem(4, both),
            sem(4, both), sem(4, both), sem(4), sem(4), sem(4), sem(4), sem(2, 4), sem(2, 4),
        ],
        compiler_params=pltpu.CompilerParams(
            collective_id=0, has_side_effects=True, vmem_limit_bytes=LIMIT
        ),
    )(*entries(global_ids, random_ids, random_count), kvq, out_grad, w)
    grads = [jnp.transpose(g.reshape(HPD, HERE, HD), (1, 0, 2)) for g in (dqh, dkh, dvh)]
    return (projected, *grads)


def solution(mesh):
    placed = (
        P("ctx", "head", None),
        P("ctx", "head", None),
        P("ctx", "head", None),
        P("head", None, None),
        P("ctx", "head"),
        P(),
        P(),
        P(),
    )
    return jax.shard_map(
        local,
        mesh=mesh,
        in_specs=placed,
        out_specs=(
            P("ctx", "head"),
            P("ctx", "head", None),
            P("ctx", "head", None),
            P("ctx", "head", None),
        ),
        check_vma=False,
    )
```

```python
import functools
import math

import jax
import jax.numpy as jnp
from jax import lax
from jax.experimental import pallas as pl
from jax.experimental.pallas import tpu as pltpu
from jax.sharding import PartitionSpec as P

SIDE = 4
BLOCK = 64
G = 2
R = 3
HERE = 640
NBD = 10
HD = 128
HPD = 4
NB = 160
SHARD = 512
MESH = pl.DeviceIdType.MESH
NT = (((1,), (1,)), ((), ()))
TN = (((0,), (0,)), ((), ()))


def place():
    ctx, hd = lax.axis_index("ctx"), lax.axis_index("head")
    return ctx, hd, ctx // SIDE, lax.rem(ctx, SIDE), hd // 2, lax.rem(hd, 2)


def query_row(y, c):
    return y * (1 - c) + (3 - y) * c


def remote(src, dst, send, recv, device):
    return pltpu.make_async_remote_copy(
        src_ref=src, dst_ref=dst, send_sem=send, recv_sem=recv, device_id=device, device_id_type=MESH
    )


def greet(device):
    pl.semaphore_signal(pltpu.get_barrier_semaphore(), inc=1, device_id=device, device_id_type=MESH)


def blocks_of(index):
    return pl.ds(index * NBD, NBD)


PIECES = 1
PIECE = HERE // PIECES
CUT = NBD // PIECES


def padded(index, h):
    return pl.ds(1 + index * NBD + h * CUT, CUT)


def pieces(*refs):
    return [(t * PIECES + h, h, t, ref) for h in range(PIECES) for t, ref in enumerate(refs)]


def neighbours(x, y, z, c):
    pair = {"ctx": x * SIDE + y + 1 - 2 * lax.rem(y, 2)}
    other = {"head": 2 * z + 1 - c}
    up = {"head": 2 * lax.rem(z + 1, SIDE) + c}
    down = {"head": 2 * lax.rem(z + 3, SIDE) + c}
    return pair, other, up, down


def enter(senders, to_self):
    for device, mine in senders:
        if mine is None:
            greet(device)
        else:
            pl.when(jnp.logical_not(mine))(functools.partial(greet, device))
    pl.semaphore_wait(pltpu.get_barrier_semaphore(), len(senders) - to_self)


class Sends:
    def __init__(self):
        self.started, self.guarded = [], []

    def start(self, copy):
        copy.start()
        self.started.append(copy)

    def start_unless(self, mine, src, dst, send, recv, device):
        copy = remote(src, dst, send, recv, device)
        here = pltpu.make_async_copy(src, dst, recv)
        pl.when(jnp.logical_not(mine))(copy.start)
        pl.when(mine)(here.start)
        self.guarded.append((copy, mine))

    def wait(self):
        for copy in self.started:
            copy.wait_send()
        for copy, mine in self.guarded:
            pl.when(jnp.logical_not(mine))(copy.wait_send)


QUARTER = HERE // 4


def quarter(q):
    return pl.ds(q * QUARTER, QUARTER)


UNROLL = 5
MASKED = -1e30
NR = 4 * NBD * R
LAST = NR + G
LISTED = LAST + NB


def layer_kernel(
    aux, off, kvq, og, w, proj, dqh, dkh, dvh,
    ka, va, qa, doa, oa, dqa, ogv, acc, dov, wv, dka, dva, dkg, dvg, runk, runv,
    oh, core_in, hop_in, z_in, stage, dcore, psend, nsend, dpair,
    ks, kr, qs, qr, ps, pr, fs, fr, ds, dr, zs, zr, cs, cr, own, wsem,
    os, orr, gs, gr, es, er, bs, br, hs, hr, c2s, c2r, as_, ar, z2s, z2r,
):
    ctx, hd, x, y, z, c = place()
    f32, bf16 = jnp.float32, jnp.bfloat16
    half = y // 2
    pair, other, up, down = neighbours(x, y, z, c)
    cw = lax.rem(half + c, 2)
    yw = query_row(y, cw)
    py = y + 1 - 2 * lax.rem(y, 2)
    near, pair_near = query_row(y, c), query_row(py, c)
    other_near, other_pair_near = query_row(y, 1 - c), query_row(py, 1 - c)
    to_self = 1 - jnp.minimum(c + half, 1)
    me = to_self == 1

    def worker(k):
        return {"ctx": k * SIDE + yw, "head": 2 * z + cw}

    senders = [
        ({"ctx": lax.rem(x + dx, SIDE) * SIDE + near, "head": 2 * z + half}, None if dx else me)
        for dx in range(SIDE)
    ]
    local = pltpu.make_async_copy(og, ogv.at[hd], own)
    local.start()
    weight = pltpu.make_async_copy(w, wv, wsem)
    weight.start()
    receivers = [
        ({"ctx": lax.rem(x + dx, SIDE) * SIDE + yw, "head": 2 * z + cw}, None if dx else me)
        for dx in range(SIDE)
    ]
    enter(senders + receivers + [(up, None), (down, None), (other, None), (pair, None)], 2 * to_self)

    sends, early = Sends(), Sends()

    def send_worker(src, dst, send, recv, dx, k):
        if dx:
            sends.start(remote(src, dst, send, recv, worker(k)))
        else:
            sends.start_unless(me, src, dst, send, recv, worker(k))

    def arrived(view, recv):
        remote(view, view, recv, recv, other).wait_recv()

    def send_pieces(dxs):
        for m, h, t, dst in pieces(ka, va):
            for dx in dxs:
                k = lax.rem(x + dx, SIDE)
                src = kvq.at[k, t, pl.ds(h * CUT, CUT)]
                send_worker(src, dst.at[padded(ctx, h)], ks.at[dx, m], kr.at[x, m], dx, k)

    send_pieces((0,))
    for q in range(4):
        for i, to, p in ((0, up, q), (1, down, (q + 2) % 4)):
            sends.start(remote(og.at[quarter(p)], ogv.at[hd, quarter(p)], zs.at[i, p], zr.at[i, p], to))
    send_pieces((1, 3))
    sends.start(remote(og, ogv.at[hd], cs.at[0], cr.at[0], other))
    dka[...] = jnp.zeros_like(dka)
    dva[...] = jnp.zeros_like(dva)
    for ref in (dkg, dvg):
        ref[...] = jnp.zeros_like(ref)
    for ref in (ka, va):
        ref[0] = jnp.zeros((BLOCK, HD), bf16)
        ref[NB + 1] = jnp.zeros((BLOCK, HD), bf16)
    for ref in (runk, runv):
        ref[0] = jnp.zeros((BLOCK, HD), f32)

    def add_shard(s):
        columns = pl.ds(pl.multiple_of(s * SHARD, SHARD), SHARD)

        def tile(i, carry):
            part = pl.ds(pl.multiple_of(i * PIECE, PIECE), PIECE)
            acc[part, :] += lax.dot_general(
                ogv[s, part, :], wv[:, columns], NT, preferred_element_type=f32
            )
            return carry

        lax.fori_loop(0, PIECES, tile, 0)

    def pass_near(dxs):
        for m, h, t, dst in pieces(ka, va):
            for dx in dxs:
                xs = lax.rem(x + SIDE - dx, SIDE)
                view = dst.at[padded(xs * SIDE + near, h)]
                arrived(view, kr.at[xs, m])
                sends.start(remote(view, view, ps.at[xs, m], pr.at[xs, m], pair))
                sends.start(remote(view, view, fs.at[xs, m], fr.at[xs, m], other))

    def pass_pair(dx):
        xs = lax.rem(x + SIDE - dx, SIDE)
        for m, h, t, dst in pieces(ka, va):
            view = dst.at[padded(xs * SIDE + pair_near, h)]
            arrived(view, pr.at[xs, m])
            sends.start(remote(view, view, fs.at[4 + xs, m], fr.at[4 + xs, m], other))

    below = 2 * lax.rem(z + 3, SIDE)
    above = 2 * lax.rem(z + 1, SIDE)
    across = 2 * lax.rem(z + 2, SIDE)

    pass_near((0,))
    for q in range(2):
        for i, s, to, p in ((0, below, up, q), (1, above, down, q + 2)):
            view = ogv.at[s + c, quarter(p)]
            arrived(view, zr.at[i, p])
            early.start(remote(view, view, zs.at[2, p], zr.at[2, p], to))
    pass_near((1, 3))
    send_pieces((2,))
    for dx in (0, 1, 3, 2):
        k = lax.rem(x + dx, SIDE)
        send_worker(kvq.at[k, 2], qa.at[blocks_of(x)], qs.at[dx], qr.at[x], dx, k)
    acc[...] = jnp.zeros_like(acc)
    local.wait()
    weight.wait()
    add_shard(hd)
    arrived(ogv.at[2 * z + 1 - c], cr.at[0])
    add_shard(2 * z + 1 - c)
    pass_near((2,))
    pass_pair(0)
    for i, s in ((0, below), (1, above)):
        for q in range(2):
            p = q + 2 - 2 * i
            arrived(ogv.at[s + c, quarter(p)], zr.at[i, p])
        early.start(remote(ogv.at[s + c], ogv.at[s + c], cs.at[1 + i], cr.at[1 + i], other))
        add_shard(s + c)
    for i, s in ((0, below), (1, above)):
        arrived(ogv.at[s + 1 - c], cr.at[1 + i])
        add_shard(s + 1 - c)
    pass_pair(1)
    for p in range(4):
        arrived(ogv.at[across + c, quarter(p)], zr.at[2, p])
    early.start(remote(ogv.at[across + c], ogv.at[across + c], cs.at[3], cr.at[3], other))
    add_shard(across + c)
    arrived(ogv.at[across + 1 - c], cr.at[3])
    add_shard(across + 1 - c)
    for k in range(HPD):
        dov[k] = acc[:, k * HD : (k + 1) * HD].astype(bf16).reshape(NBD, BLOCK, HD)
    for dx in (2, 1, 3, 0):
        k = lax.rem(x + dx, SIDE)
        send_worker(dov.at[k], doa.at[blocks_of(x)], ds.at[dx], dr.at[x], dx, k)
    pass_pair(3)
    pass_pair(2)
    for xs in range(SIDE):
        arrived(qa.at[blocks_of(xs)], qr.at[xs])
        arrived(doa.at[blocks_of(xs)], dr.at[xs])
        for m, h, t, dst in pieces(ka, va):
            arrived(dst.at[padded(xs * SIDE + other_near, h)], fr.at[xs, m])
            arrived(dst.at[padded(xs * SIDE + other_pair_near, h)], fr.at[4 + xs, m])

    scale = 1.0 / math.sqrt(HD)

    def named(entry):
        return aux[LISTED + entry]

    g0, g1 = named(NR), named(NR + 1)
    column = lax.broadcasted_iota(jnp.int32, (1, 8 * BLOCK), 1) // BLOCK
    entry_is = [jnp.where(column == j, 1.0, 0.0).astype(f32) for j in range(8)]

    def listed(ref, window, randoms):
        near_rows = ref[window].reshape(3 * BLOCK, HD)
        return jnp.concatenate([near_rows, ref[g0], ref[g1]] + [ref[r] for r in randoms], axis=0)

    def step(turn, xs, m):
        work = []
        for u in range(UNROLL):
            block = m * UNROLL + u
            n = turn * NBD + block
            i = (xs * SIDE + near) * NBD + block
            bias = entry_is[0] * jnp.where(i == 0, MASKED, 0.0) + entry_is[2] * jnp.where(i == NB - 1, MASKED, 0.0)
            for r in range(R):
                bias = bias + entry_is[5 + r] * off[n * R + r]
            randoms = [named(n * R + r) for r in range(R)]
            work.append((xs * NBD + block, pl.ds(i, 3), randoms, bias, n))
        kc = [listed(ka, t[1], t[2]) for t in work]
        vc = [listed(va, t[1], t[2]) for t in work]
        qn = [qa[t[0]] for t in work]
        dn = [doa[t[0]] for t in work]
        s = [
            lax.dot_general(a, b, NT, preferred_element_type=f32) * scale + t[3]
            for a, b, t in zip(qn, kc, work)
        ]
        dp = [lax.dot_general(a, b, NT, preferred_element_type=f32) for a, b in zip(dn, vc)]
        e = [jnp.exp(a - jnp.max(a, axis=1, keepdims=True)) for a in s]
        p = [a * (1.0 / jnp.sum(a, axis=1, keepdims=True)) for a in e]
        low_p = [a.astype(bf16) for a in p]
        on = [jnp.dot(a, b, preferred_element_type=f32).astype(bf16) for a, b in zip(low_p, vc)]
        delta = [
            jnp.sum(a.astype(f32) * b.astype(f32), axis=1, keepdims=True) for a, b in zip(dn, on)
        ]
        dsc = [(a * (b - d)).astype(bf16) for a, b, d in zip(p, dp, delta)]
        dvt = [lax.dot_general(a, b, TN, preferred_element_type=f32) for a, b in zip(low_p, dn)]
        dkt = [lax.dot_general(a, b, TN, preferred_element_type=f32) for a, b in zip(dsc, qn)]
        dqn = [
            (jnp.dot(a, b, preferred_element_type=f32) * scale).astype(bf16) for a, b in zip(dsc, kc)
        ]
        for t, a, b in zip(work, on, dqn):
            oa[t[0]] = a
            dqa[t[0]] = b
        for total, glob, run, terms in ((dka, dkg, runk, dkt), (dva, dvg, runv, dvt)):
            glob[...] += sum(a[3 * BLOCK : 5 * BLOCK] for a in terms).reshape(G, BLOCK, HD)
            for t, a in zip(work, terms):
                total[t[1]] += a[: 3 * BLOCK].reshape(3, BLOCK, HD)
                for r in range(R):
                    entry = t[4] * R + r
                    run[entry + 1] = a[(5 + r) * BLOCK : (6 + r) * BLOCK] + run[aux[entry]]

    def home_of(xs):
        return {"ctx": xs * SIDE + near, "head": 2 * z + half}

    def source_turn(turn, carry):
        xs = lax.rem(x + turn + 1, SIDE)

        def half_turn(m, inner):
            step(turn, xs, m)
            return inner

        lax.fori_loop(0, NBD // UNROLL, half_turn, 0)
        mine = me & (turn == SIDE - 1)
        copy = remote(oa.at[blocks_of(xs)], oh.at[x], os.at[turn], orr.at[x], home_of(xs))
        here = pltpu.make_async_copy(oa.at[blocks_of(xs)], oh.at[x], orr.at[x])
        pl.when(jnp.logical_not(mine))(copy.start)
        pl.when(mine)(here.start)
        return carry

    lax.fori_loop(0, SIDE, source_turn, 0)
    for i in range(SIDE):
        xs = lax.rem(x + i + 1, SIDE)
        copy = remote(oa.at[blocks_of(xs)], oh.at[x], os.at[i], orr.at[x], home_of(xs))
        if i < SIDE - 1:
            sends.started.append(copy)
        else:
            sends.guarded.append((copy, me))
    for run, glob in ((runk, dkg), (runv, dvg)):
        for i in range(G):
            run[NR + i + 1] = glob[i] + run[aux[NR + i]]
    early.wait()

    def put_sum(ref, j, t, h, total, run, index, factor, also):
        def block(n, carry):
            here = h * CUT + n
            u = index * NBD + here
            value = (total[u + 1] + run[aux[LAST + u]]) * factor
            for other_ref, slot in also:
                value = value + other_ref[slot, t, here].astype(f32)
            ref[j, t, here] = value.astype(bf16)
            return carry

        lax.fori_loop(0, CUT, block, 0)

    totals = ((dka, runk, scale), (dva, runv, 1.0))

    def part(h):
        return pl.ds(h * CUT, CUT)

    def for_other_core(g, there, dx):
        xs = lax.rem(x + dx, SIDE)
        for m, h, t, (total, run, factor) in pieces(*totals):
            put_sum(stage, g + xs, t, h, total, run, xs * SIDE + there, factor, ())
            sends.start(
                remote(stage.at[g + xs, t, part(h)], dcore.at[g + xs, t, part(h)], es.at[g + xs, m], er.at[g + xs, m], other)
            )

    def for_pair(dx):
        xs = lax.rem(x + dx, SIDE)
        for m, h, t, (total, run, factor) in pieces(*totals):
            arrived(dcore.at[xs, t, part(h)], er.at[xs, m])
            put_sum(psend, xs, t, h, total, run, xs * SIDE + pair_near, factor, ((dcore, xs),))
            sends.start(
                remote(psend.at[xs, t, part(h)], dpair.at[xs, t, part(h)], bs.at[xs, m], br.at[xs, m], pair)
            )

    def finish(dx):
        xs = lax.rem(x + dx, SIDE)
        for m, h, t, (total, run, factor) in pieces(*totals):
            arrived(dcore.at[4 + xs, t, part(h)], er.at[4 + xs, m])
            arrived(dpair.at[xs, t, part(h)], br.at[xs, m])
            put_sum(
                nsend, xs, t, h, total, run, xs * SIDE + near, factor, ((dcore, 4 + xs), (dpair, xs))
            )
            src, dst = nsend.at[xs, t, part(h)], (dkh, dvh)[t].at[x, part(h)]
            if dx:
                sends.start(remote(src, dst, hs.at[dx, m], hr.at[x, m], home_of(xs)))
            else:
                sends.start_unless(me, src, dst, hs.at[dx, m], hr.at[x, m], home_of(xs))

    for dx in (2, 1, 3, 0):
        for_other_core(0, other_pair_near, dx)
    for_pair(2)
    for_pair(1)
    for k in range(HPD):
        arrived(oh.at[k], orr.at[k])
    for i in range(SIDE):
        xs = lax.rem(x + i + 1, SIDE)
        args = dqa.at[blocks_of(xs)], dqh.at[x], gs.at[i], gr.at[x], home_of(xs)
        if i < SIDE - 1:
            sends.start(remote(*args))
        else:
            sends.start_unless(me, *args)

    def shard_product(s, put):
        columns = pl.ds(pl.multiple_of(s * SHARD, SHARD), SHARD)

        def tile(i, carry):
            rows = pl.ds(pl.multiple_of(i * PIECE, PIECE), PIECE)
            left = [oh[k, pl.ds(i * CUT, CUT)].reshape(PIECE, HD) for k in range(HPD)]
            left = jnp.concatenate(left, axis=1)
            put(rows, jnp.dot(left, wv[:, columns], preferred_element_type=f32))
            return carry

        lax.fori_loop(0, PIECES, tile, 0)

    for i, s in enumerate((across, above, below, 2 * z)):

        def put(rows, value):
            ogv[i, rows, :] = value.astype(bf16)

        shard_product(s + 1 - c, put)
        sends.start(remote(ogv.at[i], core_in.at[i], c2s.at[i], c2r.at[i], other))

    arrived(core_in.at[0], c2r.at[0])

    def put_across(rows, value):
        ogv[4, rows, :] = (value + core_in[0, rows, :].astype(f32)).astype(bf16)

    shard_product(across + c, put_across)
    for q in range(4):
        sends.start(
            remote(
                ogv.at[4, quarter(q)], hop_in.at[quarter(q)], as_.at[q], ar.at[q], up if q < 2 else down
            )
        )
    for i, s, to in ((0, above, up), (1, below, down)):
        arrived(core_in.at[1 + i], c2r.at[1 + i])

        def put_near(rows, value):
            ogv[5 + i, rows, :] = (value + core_in[1 + i, rows, :].astype(f32)).astype(bf16)

        shard_product(s + c, put_near)
        for q in (2 - 2 * i, 3 - 2 * i):
            sends.start(
                remote(ogv.at[5 + i, quarter(q)], z_in.at[i, quarter(q)], z2s.at[i, q], z2r.at[i, q], to)
            )
    arrived(core_in.at[3], c2r.at[3])

    def put_own(rows, value):
        acc[rows, :] = value + core_in[3, rows, :].astype(f32)

    for_pair(3)
    for_pair(0)
    for dx in (2, 1, 3, 0):
        for_other_core(4, other_near, dx)
    shard_product(hd, put_own)
    for q in range(2):
        for i, to in ((0, up), (1, down)):
            p = q + 2 * i
            arrived(hop_in.at[quarter(p)], ar.at[p])
            ogv[5 + i, quarter(p), :] = (
                ogv[5 + i, quarter(p), :].astype(f32) + hop_in[quarter(p), :].astype(f32)
            ).astype(bf16)
            sends.start(
                remote(ogv.at[5 + i, quarter(p)], z_in.at[i, quarter(p)], z2s.at[i, p], z2r.at[i, p], to)
            )
    for dx in (2, 1, 3, 0):
        finish(dx)
    for i in range(2):
        for q in range(4):
            arrived(z_in.at[i, quarter(q)], z2r.at[i, q])
    proj[...] = (acc[...] + z_in[0].astype(f32) + z_in[1].astype(f32)).astype(bf16)
    for k in range(HPD):
        arrived(dqh.at[k], gr.at[k])
        for m, h, t, out in pieces(dkh, dvh):
            arrived(out.at[k, part(h)], hr.at[k, m])
    sends.wait()


ANY = pl.BlockSpec(memory_space=pl.ANY)
VMEM = pl.BlockSpec(memory_space=pltpu.VMEM)
SMEM = pl.BlockSpec(memory_space=pltpu.SMEM)
LIMIT = 60 * 1024 * 1024


def struct(*shape):
    return jax.ShapeDtypeStruct(shape, jnp.bfloat16)


def sem(*shape):
    return pltpu.SemaphoreType.DMA(shape)


def prepare_kernel(rid, cnt, gid, k, v, q, kvq, aux, off):
    _, _, x, y, _, c = place()
    near = query_row(y, c)

    def clear(b, carry):
        aux[LAST + b] = 0
        return carry

    lax.fori_loop(0, NB, clear, 0, unroll=8)

    def enter_block(entry, block):
        aux[entry] = aux[LAST + block]
        aux[LAST + block] = entry + 1
        aux[LISTED + entry] = block + 1

    for turn in range(SIDE):
        first = (lax.rem(x + turn + 1, SIDE) * SIDE + near) * NBD

        def query_block(b, carry):
            i = first + b
            for r in range(R):
                entry = (turn * NBD + b) * R + r
                enter_block(entry, rid[r, i])
                off[entry] = jnp.where(r < cnt[i], 0.0, MASKED).astype(jnp.float32)
            if turn < 3:
                rows = (k, v, q)[turn][pl.ds(b * BLOCK, BLOCK)]
                kvq[:, turn, b] = jnp.swapaxes(rows, 0, 1)
            return carry

        lax.fori_loop(0, NBD, query_block, 0)
    for g in range(G):
        enter_block(NR + g, gid[g])


def finish_kernel(dqh, dkh, dvh, summed, dq, dk, dv, projected):
    projected[...] = summed[...]
    for ref, out in ((dqh, dq), (dkh, dk), (dvh, dv)):
        out[...] = jnp.swapaxes(ref[...].reshape(HPD, HERE, HD), 0, 1)


def local(queries, key_rows, value_rows, out_weight, out_grad, global_ids, random_ids, random_count):
    bf16, f32 = jnp.bfloat16, jnp.float32
    kvq, aux, off = pl.pallas_call(
        prepare_kernel,
        out_shape=(
            struct(HPD, 3, NBD, BLOCK, HD),
            jax.ShapeDtypeStruct((LISTED + NR + G,), jnp.int32),
            jax.ShapeDtypeStruct((NR,), jnp.float32),
        ),
        in_specs=[SMEM] * 3 + [VMEM] * 3,
        out_specs=(VMEM, SMEM, SMEM),
        compiler_params=pltpu.CompilerParams(vmem_limit_bytes=LIMIT),
    )(random_ids.T, random_count, global_ids, key_rows, value_rows, queries)
    w = out_weight.reshape(HPD * HD, out_weight.shape[2])
    both = 2 * PIECES

    def vmem(*shape, dtype=bf16):
        return pltpu.VMEM(shape, dtype)

    def blocks(*count, dtype=bf16):
        return vmem(*count, BLOCK, HD, dtype=dtype)

    one = pltpu.SemaphoreType.DMA
    summed, dqh, dkh, dvh = pl.pallas_call(
        layer_kernel,
        out_shape=(struct(HERE, SHARD),) + (struct(HPD, NBD, BLOCK, HD),) * 3,
        in_specs=[SMEM, SMEM, ANY, ANY, ANY],
        out_specs=(VMEM, ANY, ANY, ANY),
        scratch_shapes=[
            blocks(NB + 2), blocks(NB + 2), blocks(4 * NBD), blocks(4 * NBD), blocks(4 * NBD), blocks(4 * NBD),
            vmem(8, HERE, SHARD), vmem(HERE, SHARD, dtype=f32), blocks(HPD, NBD), vmem(*w.shape),
            blocks(NB + 2, dtype=f32), blocks(NB + 2, dtype=f32), blocks(G, dtype=f32), blocks(G, dtype=f32),
            blocks(NR + G + 1, dtype=f32), blocks(NR + G + 1, dtype=f32),
            blocks(HPD, NBD), vmem(4, HERE, SHARD), vmem(HERE, SHARD), vmem(2, HERE, SHARD),
            blocks(8, 2, NBD), blocks(8, 2, NBD), blocks(4, 2, NBD), blocks(4, 2, NBD), blocks(4, 2, NBD),
            sem(4, both), sem(4, both), sem(4), sem(4), sem(4, both), sem(4, both), sem(8, both), sem(8, both),
            sem(4), sem(4), sem(3, 4), sem(3, 4), sem(4), sem(4), one, one,
            sem(4), sem(4), sem(4), sem(4), sem(8, both), sem(8, both), sem(4, both), sem(4, both),
            sem(4, both), sem(4, both), sem(4), sem(4), sem(4), sem(4), sem(2, 4), sem(2, 4),
        ],
        compiler_params=pltpu.CompilerParams(
            collective_id=0, has_side_effects=True, vmem_limit_bytes=LIMIT
        ),
    )(aux, off, kvq, out_grad, w)
    *grads, projected = pl.pallas_call(
        finish_kernel,
        out_shape=(struct(HERE, HPD, HD),) * 3 + (struct(HERE, SHARD),),
        in_specs=[VMEM] * 4,
        out_specs=(VMEM,) * 4,
        compiler_params=pltpu.CompilerParams(vmem_limit_bytes=LIMIT),
    )(dqh, dkh, dvh, summed)
    return (projected, *grads)


def solution(mesh):
    placed = (
        P("ctx", "head", None),
        P("ctx", "head", None),
        P("ctx", "head", None),
        P("head", None, None),
        P("ctx", "head"),
        P(),
        P(),
        P(),
    )
    return jax.shard_map(
        local,
        mesh=mesh,
        in_specs=placed,
        out_specs=(
            P("ctx", "head"),
            P("ctx", "head", None),
            P("ctx", "head", None),
            P("ctx", "head", None),
        ),
        check_vma=False,
    )
```

```python
import functools
import math

import jax
import jax.numpy as jnp
from jax import lax
from jax.experimental import pallas as pl
from jax.experimental.pallas import tpu as pltpu
from jax.sharding import PartitionSpec as P

SIDE = 4
BLOCK = 64
G = 2
R = 3
HERE = 640
NBD = 10
HD = 128
HPD = 4
NB = 160
SHARD = 512
MESH = pl.DeviceIdType.MESH
NT = (((1,), (1,)), ((), ()))
TN = (((0,), (0,)), ((), ()))


def place():
    ctx, hd = lax.axis_index("ctx"), lax.axis_index("head")
    return ctx, hd, ctx // SIDE, lax.rem(ctx, SIDE), hd // 2, lax.rem(hd, 2)


def query_row(y, c):
    return y * (1 - c) + (3 - y) * c


def remote(src, dst, send, recv, device):
    return pltpu.make_async_remote_copy(
        src_ref=src, dst_ref=dst, send_sem=send, recv_sem=recv, device_id=device, device_id_type=MESH
    )


def greet(device):
    pl.semaphore_signal(pltpu.get_barrier_semaphore(), inc=1, device_id=device, device_id_type=MESH)


def blocks_of(index):
    return pl.ds(index * NBD, NBD)


PIECES = 1
PIECE = HERE // PIECES
CUT = NBD // PIECES


def padded(index, h):
    return pl.ds(1 + index * NBD + h * CUT, CUT)


def pieces(*refs):
    return [(t * PIECES + h, h, t, ref) for h in range(PIECES) for t, ref in enumerate(refs)]


def neighbours(x, y, z, c):
    pair = {"ctx": x * SIDE + y + 1 - 2 * lax.rem(y, 2)}
    other = {"head": 2 * z + 1 - c}
    up = {"head": 2 * lax.rem(z + 1, SIDE) + c}
    down = {"head": 2 * lax.rem(z + 3, SIDE) + c}
    return pair, other, up, down


def enter(senders, to_self):
    for device, mine in senders:
        if mine is None:
            greet(device)
        else:
            pl.when(jnp.logical_not(mine))(functools.partial(greet, device))
    pl.semaphore_wait(pltpu.get_barrier_semaphore(), len(senders) - to_self)


class Sends:
    def __init__(self):
        self.started, self.guarded = [], []

    def start(self, copy):
        copy.start()
        self.started.append(copy)

    def start_unless(self, mine, src, dst, send, recv, device):
        copy = remote(src, dst, send, recv, device)
        here = pltpu.make_async_copy(src, dst, recv)
        pl.when(jnp.logical_not(mine))(copy.start)
        pl.when(mine)(here.start)
        self.guarded.append((copy, mine))

    def wait(self):
        for copy in self.started:
            copy.wait_send()
        for copy, mine in self.guarded:
            pl.when(jnp.logical_not(mine))(copy.wait_send)


QUARTER = HERE // 4


def quarter(q):
    return pl.ds(q * QUARTER, QUARTER)


UNROLL = 5
MASKED = -1e30
NR = 4 * NBD * R
LAST = NR + G
LISTED = LAST + NB


def layer_kernel(
    aux, off, kvq, og, w, proj, dqh, dkh, dvh,
    ka, va, qa, doa, oa, dqa, probs, ogv, acc, dov, wv, dka, dva, dkg, dvg, runk, runv,
    oh, core_in, hop_in, z_in, stage, dcore, psend, nsend, dpair,
    ks, kr, qs, qr, ps, pr, fs, fr, ds, dr, zs, zr, cs, cr, own, wsem,
    os, orr, gs, gr, es, er, bs, br, hs, hr, c2s, c2r, as_, ar, z2s, z2r,
):
    ctx, hd, x, y, z, c = place()
    f32, bf16 = jnp.float32, jnp.bfloat16
    half = y // 2
    pair, other, up, down = neighbours(x, y, z, c)
    cw = lax.rem(half + c, 2)
    yw = query_row(y, cw)
    py = y + 1 - 2 * lax.rem(y, 2)
    near, pair_near = query_row(y, c), query_row(py, c)
    other_near, other_pair_near = query_row(y, 1 - c), query_row(py, 1 - c)
    to_self = 1 - jnp.minimum(c + half, 1)
    me = to_self == 1

    def worker(k):
        return {"ctx": k * SIDE + yw, "head": 2 * z + cw}

    senders = [
        ({"ctx": lax.rem(x + dx, SIDE) * SIDE + near, "head": 2 * z + half}, None if dx else me)
        for dx in range(SIDE)
    ]
    local = pltpu.make_async_copy(og, ogv.at[hd], own)
    local.start()
    weight = pltpu.make_async_copy(w, wv, wsem)
    weight.start()
    receivers = [
        ({"ctx": lax.rem(x + dx, SIDE) * SIDE + yw, "head": 2 * z + cw}, None if dx else me)
        for dx in range(SIDE)
    ]
    enter(senders + receivers + [(up, None), (down, None), (other, None), (pair, None)], 2 * to_self)

    sends, early = Sends(), Sends()

    def send_worker(src, dst, send, recv, dx, k):
        if dx:
            sends.start(remote(src, dst, send, recv, worker(k)))
        else:
            sends.start_unless(me, src, dst, send, recv, worker(k))

    def arrived(view, recv):
        remote(view, view, recv, recv, other).wait_recv()

    def send_pieces(dxs):
        for m, h, t, dst in pieces(ka, va):
            for dx in dxs:
                k = lax.rem(x + dx, SIDE)
                src = kvq.at[k, t, pl.ds(h * CUT, CUT)]
                send_worker(src, dst.at[padded(ctx, h)], ks.at[dx, m], kr.at[x, m], dx, k)

    send_pieces((0,))
    for q in range(4):
        for i, to, p in ((0, up, q), (1, down, (q + 2) % 4)):
            sends.start(remote(og.at[quarter(p)], ogv.at[hd, quarter(p)], zs.at[i, p], zr.at[i, p], to))
    send_pieces((1, 3))
    sends.start(remote(og, ogv.at[hd], cs.at[0], cr.at[0], other))
    dka[...] = jnp.zeros_like(dka)
    dva[...] = jnp.zeros_like(dva)
    for ref in (dkg, dvg):
        ref[...] = jnp.zeros_like(ref)
    for ref in (ka, va):
        ref[0] = jnp.zeros((BLOCK, HD), bf16)
        ref[NB + 1] = jnp.zeros((BLOCK, HD), bf16)
    for ref in (runk, runv):
        ref[0] = jnp.zeros((BLOCK, HD), f32)

    def add_shard(s):
        columns = pl.ds(pl.multiple_of(s * SHARD, SHARD), SHARD)

        def tile(i, carry):
            part = pl.ds(pl.multiple_of(i * PIECE, PIECE), PIECE)
            acc[part, :] += lax.dot_general(
                ogv[s, part, :], wv[:, columns], NT, preferred_element_type=f32
            )
            return carry

        lax.fori_loop(0, PIECES, tile, 0)

    def pass_near(dxs):
        for m, h, t, dst in pieces(ka, va):
            for dx in dxs:
                xs = lax.rem(x + SIDE - dx, SIDE)
                view = dst.at[padded(xs * SIDE + near, h)]
                arrived(view, kr.at[xs, m])
                sends.start(remote(view, view, ps.at[xs, m], pr.at[xs, m], pair))
                sends.start(remote(view, view, fs.at[xs, m], fr.at[xs, m], other))

    def pass_pair(dx):
        xs = lax.rem(x + SIDE - dx, SIDE)
        for m, h, t, dst in pieces(ka, va):
            view = dst.at[padded(xs * SIDE + pair_near, h)]
            arrived(view, pr.at[xs, m])
            sends.start(remote(view, view, fs.at[4 + xs, m], fr.at[4 + xs, m], other))

    below = 2 * lax.rem(z + 3, SIDE)
    above = 2 * lax.rem(z + 1, SIDE)
    across = 2 * lax.rem(z + 2, SIDE)

    pass_near((0,))
    for q in range(2):
        for i, s, to, p in ((0, below, up, q), (1, above, down, q + 2)):
            view = ogv.at[s + c, quarter(p)]
            arrived(view, zr.at[i, p])
            early.start(remote(view, view, zs.at[2, p], zr.at[2, p], to))
    pass_near((1, 3))
    send_pieces((2,))
    for dx in (0, 1, 3, 2):
        k = lax.rem(x + dx, SIDE)
        send_worker(kvq.at[k, 2], qa.at[blocks_of(x)], qs.at[dx], qr.at[x], dx, k)
    acc[...] = jnp.zeros_like(acc)
    local.wait()
    weight.wait()
    add_shard(hd)
    arrived(ogv.at[2 * z + 1 - c], cr.at[0])
    add_shard(2 * z + 1 - c)
    pass_near((2,))
    pass_pair(0)
    for i, s in ((0, below), (1, above)):
        for q in range(2):
            p = q + 2 - 2 * i
            arrived(ogv.at[s + c, quarter(p)], zr.at[i, p])
        early.start(remote(ogv.at[s + c], ogv.at[s + c], cs.at[1 + i], cr.at[1 + i], other))
        add_shard(s + c)
    for i, s in ((0, below), (1, above)):
        arrived(ogv.at[s + 1 - c], cr.at[1 + i])
        add_shard(s + 1 - c)
    pass_pair(1)
    for p in range(4):
        arrived(ogv.at[across + c, quarter(p)], zr.at[2, p])
    early.start(remote(ogv.at[across + c], ogv.at[across + c], cs.at[3], cr.at[3], other))
    add_shard(across + c)
    arrived(ogv.at[across + 1 - c], cr.at[3])
    add_shard(across + 1 - c)
    for k in range(HPD):
        dov[k] = acc[:, k * HD : (k + 1) * HD].astype(bf16).reshape(NBD, BLOCK, HD)
    for dx in (2, 1, 3, 0):
        k = lax.rem(x + dx, SIDE)
        send_worker(dov.at[k], doa.at[blocks_of(x)], ds.at[dx], dr.at[x], dx, k)
    pass_pair(3)
    pass_pair(2)
    for xs in range(SIDE):
        arrived(qa.at[blocks_of(xs)], qr.at[xs])
        for m, h, t, dst in pieces(ka, va):
            arrived(dst.at[padded(xs * SIDE + other_near, h)], fr.at[xs, m])
            arrived(dst.at[padded(xs * SIDE + other_pair_near, h)], fr.at[4 + xs, m])

    scale = 1.0 / math.sqrt(HD)

    def named(entry):
        return aux[LISTED + entry]

    g0, g1 = named(NR), named(NR + 1)
    column = lax.broadcasted_iota(jnp.int32, (1, 8 * BLOCK), 1) // BLOCK
    entry_is = [jnp.where(column == j, 1.0, 0.0).astype(f32) for j in range(8)]

    def listed(ref, window, randoms):
        near_rows = ref[window].reshape(3 * BLOCK, HD)
        return jnp.concatenate([near_rows, ref[g0], ref[g1]] + [ref[r] for r in randoms], axis=0)

    def work_of(turn, xs, m):
        for u in range(UNROLL):
            block = m * UNROLL + u
            n = turn * NBD + block
            i = (xs * SIDE + near) * NBD + block
            yield n, xs * NBD + block, i, pl.ds(i, 3), [named(n * R + r) for r in range(R)]

    def forward(turn, xs, m):
        work, biases = list(work_of(turn, xs, m)), []
        for n, _, i, _, _ in work:
            bias = entry_is[0] * jnp.where(i == 0, MASKED, 0.0) + entry_is[2] * jnp.where(i == NB - 1, MASKED, 0.0)
            for r in range(R):
                bias = bias + entry_is[5 + r] * off[n * R + r]
            biases.append(bias)
        kc = [listed(ka, t[3], t[4]) for t in work]
        vc = [listed(va, t[3], t[4]) for t in work]
        qn = [qa[t[1]] for t in work]
        s = [
            lax.dot_general(a, b, NT, preferred_element_type=f32) * scale + bias
            for a, b, bias in zip(qn, kc, biases)
        ]
        e = [jnp.exp(a - jnp.max(a, axis=1, keepdims=True)) for a in s]
        low_p = [(a * (1.0 / jnp.sum(a, axis=1, keepdims=True))).astype(bf16) for a in e]
        on = [jnp.dot(a, b, preferred_element_type=f32).astype(bf16) for a, b in zip(low_p, vc)]
        for t, a, b in zip(work, on, low_p):
            oa[t[1]] = a
            probs[t[1]] = b

    def backward(turn, xs, m):
        work = list(work_of(turn, xs, m))
        kc = [listed(ka, t[3], t[4]) for t in work]
        vc = [listed(va, t[3], t[4]) for t in work]
        qn = [qa[t[1]] for t in work]
        dn = [doa[t[1]] for t in work]
        low_p = [probs[t[1]] for t in work]
        dp = [lax.dot_general(a, b, NT, preferred_element_type=f32) for a, b in zip(dn, vc)]
        delta = [
            jnp.sum(a.astype(f32) * oa[t[1]].astype(f32), axis=1, keepdims=True) for a, t in zip(dn, work)
        ]
        dsc = [(a.astype(f32) * (b - d)).astype(bf16) for a, b, d in zip(low_p, dp, delta)]
        dvt = [lax.dot_general(a, b, TN, preferred_element_type=f32) for a, b in zip(low_p, dn)]
        dkt = [lax.dot_general(a, b, TN, preferred_element_type=f32) for a, b in zip(dsc, qn)]
        dqn = [
            (jnp.dot(a, b, preferred_element_type=f32) * scale).astype(bf16) for a, b in zip(dsc, kc)
        ]
        for t, a in zip(work, dqn):
            dqa[t[1]] = a
        for total, glob, run, terms in ((dka, dkg, runk, dkt), (dva, dvg, runv, dvt)):
            glob[...] += sum(a[3 * BLOCK : 5 * BLOCK] for a in terms).reshape(G, BLOCK, HD)
            for t, a in zip(work, terms):
                total[t[3]] += a[: 3 * BLOCK].reshape(3, BLOCK, HD)
                for r in range(R):
                    entry = t[0] * R + r
                    run[entry + 1] = a[(5 + r) * BLOCK : (6 + r) * BLOCK] + run[aux[entry]]

    def home_of(xs):
        return {"ctx": xs * SIDE + near, "head": 2 * z + half}

    def source_turn(turn, carry):
        xs = lax.rem(x + turn + 1, SIDE)

        def half_turn(m, inner):
            forward(turn, xs, m)
            return inner

        lax.fori_loop(0, NBD // UNROLL, half_turn, 0)
        mine = me & (turn == SIDE - 1)
        copy = remote(oa.at[blocks_of(xs)], oh.at[x], os.at[turn], orr.at[x], home_of(xs))
        here = pltpu.make_async_copy(oa.at[blocks_of(xs)], oh.at[x], orr.at[x])
        pl.when(jnp.logical_not(mine))(copy.start)
        pl.when(mine)(here.start)
        return carry

    lax.fori_loop(0, SIDE, source_turn, 0)
    for xs in range(SIDE):
        arrived(doa.at[blocks_of(xs)], dr.at[xs])

    def back_turn(turn, carry):
        xs = lax.rem(x + turn + 1, SIDE)

        def half_turn(m, inner):
            backward(turn, xs, m)
            return inner

        lax.fori_loop(0, NBD // UNROLL, half_turn, 0)
        return carry

    lax.fori_loop(0, SIDE, back_turn, 0)
    for i in range(SIDE):
        xs = lax.rem(x + i + 1, SIDE)
        copy = remote(oa.at[blocks_of(xs)], oh.at[x], os.at[i], orr.at[x], home_of(xs))
        if i < SIDE - 1:
            sends.started.append(copy)
        else:
            sends.guarded.append((copy, me))
    for run, glob in ((runk, dkg), (runv, dvg)):
        for i in range(G):
            run[NR + i + 1] = glob[i] + run[aux[NR + i]]
    early.wait()

    def put_sum(ref, j, t, h, total, run, index, factor, also):
        def block(n, carry):
            here = h * CUT + n
            u = index * NBD + here
            value = (total[u + 1] + run[aux[LAST + u]]) * factor
            for other_ref, slot in also:
                value = value + other_ref[slot, t, here].astype(f32)
            ref[j, t, here] = value.astype(bf16)
            return carry

        lax.fori_loop(0, CUT, block, 0)

    totals = ((dka, runk, scale), (dva, runv, 1.0))

    def part(h):
        return pl.ds(h * CUT, CUT)

    def for_other_core(g, there, dx):
        xs = lax.rem(x + dx, SIDE)
        for m, h, t, (total, run, factor) in pieces(*totals):
            put_sum(stage, g + xs, t, h, total, run, xs * SIDE + there, factor, ())
            sends.start(
                remote(stage.at[g + xs, t, part(h)], dcore.at[g + xs, t, part(h)], es.at[g + xs, m], er.at[g + xs, m], other)
            )

    def for_pair(dx):
        xs = lax.rem(x + dx, SIDE)
        for m, h, t, (total, run, factor) in pieces(*totals):
            arrived(dcore.at[xs, t, part(h)], er.at[xs, m])
            put_sum(psend, xs, t, h, total, run, xs * SIDE + pair_near, factor, ((dcore, xs),))
            sends.start(
                remote(psend.at[xs, t, part(h)], dpair.at[xs, t, part(h)], bs.at[xs, m], br.at[xs, m], pair)
            )

    def finish(dx):
        xs = lax.rem(x + dx, SIDE)
        for m, h, t, (total, run, factor) in pieces(*totals):
            arrived(dcore.at[4 + xs, t, part(h)], er.at[4 + xs, m])
            arrived(dpair.at[xs, t, part(h)], br.at[xs, m])
            put_sum(
                nsend, xs, t, h, total, run, xs * SIDE + near, factor, ((dcore, 4 + xs), (dpair, xs))
            )
            src, dst = nsend.at[xs, t, part(h)], (dkh, dvh)[t].at[x, part(h)]
            if dx:
                sends.start(remote(src, dst, hs.at[dx, m], hr.at[x, m], home_of(xs)))
            else:
                sends.start_unless(me, src, dst, hs.at[dx, m], hr.at[x, m], home_of(xs))

    for dx in (2, 1, 3, 0):
        for_other_core(0, other_pair_near, dx)
    for_pair(2)
    for_pair(1)
    for k in range(HPD):
        arrived(oh.at[k], orr.at[k])
    for i in range(SIDE):
        xs = lax.rem(x + i + 1, SIDE)
        args = dqa.at[blocks_of(xs)], dqh.at[x], gs.at[i], gr.at[x], home_of(xs)
        if i < SIDE - 1:
            sends.start(remote(*args))
        else:
            sends.start_unless(me, *args)

    def shard_product(s, put):
        columns = pl.ds(pl.multiple_of(s * SHARD, SHARD), SHARD)

        def tile(i, carry):
            rows = pl.ds(pl.multiple_of(i * PIECE, PIECE), PIECE)
            left = [oh[k, pl.ds(i * CUT, CUT)].reshape(PIECE, HD) for k in range(HPD)]
            left = jnp.concatenate(left, axis=1)
            put(rows, jnp.dot(left, wv[:, columns], preferred_element_type=f32))
            return carry

        lax.fori_loop(0, PIECES, tile, 0)

    for i, s in enumerate((across, above, below, 2 * z)):

        def put(rows, value):
            ogv[i, rows, :] = value.astype(bf16)

        shard_product(s + 1 - c, put)
        sends.start(remote(ogv.at[i], core_in.at[i], c2s.at[i], c2r.at[i], other))

    arrived(core_in.at[0], c2r.at[0])

    def put_across(rows, value):
        ogv[4, rows, :] = (value + core_in[0, rows, :].astype(f32)).astype(bf16)

    shard_product(across + c, put_across)
    for q in range(4):
        sends.start(
            remote(
                ogv.at[4, quarter(q)], hop_in.at[quarter(q)], as_.at[q], ar.at[q], up if q < 2 else down
            )
        )
    for i, s, to in ((0, above, up), (1, below, down)):
        arrived(core_in.at[1 + i], c2r.at[1 + i])

        def put_near(rows, value):
            ogv[5 + i, rows, :] = (value + core_in[1 + i, rows, :].astype(f32)).astype(bf16)

        shard_product(s + c, put_near)
        for q in (2 - 2 * i, 3 - 2 * i):
            sends.start(
                remote(ogv.at[5 + i, quarter(q)], z_in.at[i, quarter(q)], z2s.at[i, q], z2r.at[i, q], to)
            )
    arrived(core_in.at[3], c2r.at[3])

    def put_own(rows, value):
        acc[rows, :] = value + core_in[3, rows, :].astype(f32)

    for_pair(3)
    for_pair(0)
    for dx in (2, 1, 3, 0):
        for_other_core(4, other_near, dx)
    shard_product(hd, put_own)
    for q in range(2):
        for i, to in ((0, up), (1, down)):
            p = q + 2 * i
            arrived(hop_in.at[quarter(p)], ar.at[p])
            ogv[5 + i, quarter(p), :] = (
                ogv[5 + i, quarter(p), :].astype(f32) + hop_in[quarter(p), :].astype(f32)
            ).astype(bf16)
            sends.start(
                remote(ogv.at[5 + i, quarter(p)], z_in.at[i, quarter(p)], z2s.at[i, p], z2r.at[i, p], to)
            )
    for dx in (2, 1, 3, 0):
        finish(dx)
    for i in range(2):
        for q in range(4):
            arrived(z_in.at[i, quarter(q)], z2r.at[i, q])
    proj[...] = (acc[...] + z_in[0].astype(f32) + z_in[1].astype(f32)).astype(bf16)
    for k in range(HPD):
        arrived(dqh.at[k], gr.at[k])
        for m, h, t, out in pieces(dkh, dvh):
            arrived(out.at[k, part(h)], hr.at[k, m])
    sends.wait()


ANY = pl.BlockSpec(memory_space=pl.ANY)
VMEM = pl.BlockSpec(memory_space=pltpu.VMEM)
SMEM = pl.BlockSpec(memory_space=pltpu.SMEM)
LIMIT = 60 * 1024 * 1024


def struct(*shape):
    return jax.ShapeDtypeStruct(shape, jnp.bfloat16)


def sem(*shape):
    return pltpu.SemaphoreType.DMA(shape)


def prepare_kernel(rid, cnt, gid, k, v, q, kvq, aux, off):
    _, _, x, y, _, c = place()
    near = query_row(y, c)

    def clear(b, carry):
        aux[LAST + b] = 0
        return carry

    lax.fori_loop(0, NB, clear, 0, unroll=8)

    def enter_block(entry, block):
        aux[entry] = aux[LAST + block]
        aux[LAST + block] = entry + 1
        aux[LISTED + entry] = block + 1

    for turn in range(SIDE):
        first = (lax.rem(x + turn + 1, SIDE) * SIDE + near) * NBD

        def query_block(b, carry):
            i = first + b
            for r in range(R):
                entry = (turn * NBD + b) * R + r
                enter_block(entry, rid[r, i])
                off[entry] = jnp.where(r < cnt[i], 0.0, MASKED).astype(jnp.float32)
            if turn < 3:
                rows = (k, v, q)[turn][pl.ds(b * BLOCK, BLOCK)]
                kvq[:, turn, b] = jnp.swapaxes(rows, 0, 1)
            return carry

        lax.fori_loop(0, NBD, query_block, 0)
    for g in range(G):
        enter_block(NR + g, gid[g])


def finish_kernel(dqh, dkh, dvh, summed, dq, dk, dv, projected):
    projected[...] = summed[...]
    for ref, out in ((dqh, dq), (dkh, dk), (dvh, dv)):
        out[...] = jnp.swapaxes(ref[...].reshape(HPD, HERE, HD), 0, 1)


def local(queries, key_rows, value_rows, out_weight, out_grad, global_ids, random_ids, random_count):
    bf16, f32 = jnp.bfloat16, jnp.float32
    kvq, aux, off = pl.pallas_call(
        prepare_kernel,
        out_shape=(
            struct(HPD, 3, NBD, BLOCK, HD),
            jax.ShapeDtypeStruct((LISTED + NR + G,), jnp.int32),
            jax.ShapeDtypeStruct((NR,), jnp.float32),
        ),
        in_specs=[SMEM] * 3 + [VMEM] * 3,
        out_specs=(VMEM, SMEM, SMEM),
        compiler_params=pltpu.CompilerParams(vmem_limit_bytes=LIMIT),
    )(random_ids.T, random_count, global_ids, key_rows, value_rows, queries)
    w = out_weight.reshape(HPD * HD, out_weight.shape[2])
    both = 2 * PIECES

    def vmem(*shape, dtype=bf16):
        return pltpu.VMEM(shape, dtype)

    def blocks(*count, dtype=bf16):
        return vmem(*count, BLOCK, HD, dtype=dtype)

    one = pltpu.SemaphoreType.DMA
    summed, dqh, dkh, dvh = pl.pallas_call(
        layer_kernel,
        out_shape=(struct(HERE, SHARD),) + (struct(HPD, NBD, BLOCK, HD),) * 3,
        in_specs=[SMEM, SMEM, ANY, ANY, ANY],
        out_specs=(VMEM, ANY, ANY, ANY),
        scratch_shapes=[
            blocks(NB + 2), blocks(NB + 2), blocks(4 * NBD), blocks(4 * NBD), blocks(4 * NBD), blocks(4 * NBD),
            vmem(4 * NBD, BLOCK, 8 * BLOCK),
            vmem(8, HERE, SHARD), vmem(HERE, SHARD, dtype=f32), blocks(HPD, NBD), vmem(*w.shape),
            blocks(NB + 2, dtype=f32), blocks(NB + 2, dtype=f32), blocks(G, dtype=f32), blocks(G, dtype=f32),
            blocks(NR + G + 1, dtype=f32), blocks(NR + G + 1, dtype=f32),
            blocks(HPD, NBD), vmem(4, HERE, SHARD), vmem(HERE, SHARD), vmem(2, HERE, SHARD),
            blocks(8, 2, NBD), blocks(8, 2, NBD), blocks(4, 2, NBD), blocks(4, 2, NBD), blocks(4, 2, NBD),
            sem(4, both), sem(4, both), sem(4), sem(4), sem(4, both), sem(4, both), sem(8, both), sem(8, both),
            sem(4), sem(4), sem(3, 4), sem(3, 4), sem(4), sem(4), one, one,
            sem(4), sem(4), sem(4), sem(4), sem(8, both), sem(8, both), sem(4, both), sem(4, both),
            sem(4, both), sem(4, both), sem(4), sem(4), sem(4), sem(4), sem(2, 4), sem(2, 4),
        ],
        compiler_params=pltpu.CompilerParams(
            collective_id=0, has_side_effects=True, vmem_limit_bytes=LIMIT
        ),
    )(aux, off, kvq, out_grad, w)
    *grads, projected = pl.pallas_call(
        finish_kernel,
        out_shape=(struct(HERE, HPD, HD),) * 3 + (struct(HERE, SHARD),),
        in_specs=[VMEM] * 4,
        out_specs=(VMEM,) * 4,
        compiler_params=pltpu.CompilerParams(vmem_limit_bytes=LIMIT),
    )(dqh, dkh, dvh, summed)
    return (projected, *grads)


def solution(mesh):
    placed = (
        P("ctx", "head", None),
        P("ctx", "head", None),
        P("ctx", "head", None),
        P("head", None, None),
        P("ctx", "head"),
        P(),
        P(),
        P(),
    )
    return jax.shard_map(
        local,
        mesh=mesh,
        in_specs=placed,
        out_specs=(
            P("ctx", "head"),
            P("ctx", "head", None),
            P("ctx", "head", None),
            P("ctx", "head", None),
        ),
        check_vma=False,
    )
```

```python
import functools
import math

import jax
import jax.numpy as jnp
from jax import lax
from jax.experimental import pallas as pl
from jax.experimental.pallas import tpu as pltpu
from jax.sharding import PartitionSpec as P

SIDE = 4
BLOCK = 64
G = 2
R = 3
HERE = 640
NBD = 10
HD = 128
HPD = 4
NB = 160
SHARD = 512
MESH = pl.DeviceIdType.MESH
NT = (((1,), (1,)), ((), ()))
TN = (((0,), (0,)), ((), ()))


def place():
    ctx, hd = lax.axis_index("ctx"), lax.axis_index("head")
    return ctx, hd, ctx // SIDE, lax.rem(ctx, SIDE), hd // 2, lax.rem(hd, 2)


def query_row(y, c):
    return y * (1 - c) + (3 - y) * c


def remote(src, dst, send, recv, device):
    return pltpu.make_async_remote_copy(
        src_ref=src, dst_ref=dst, send_sem=send, recv_sem=recv, device_id=device, device_id_type=MESH
    )


def greet(device):
    pl.semaphore_signal(pltpu.get_barrier_semaphore(), inc=1, device_id=device, device_id_type=MESH)


def blocks_of(index):
    return pl.ds(index * NBD, NBD)


PIECES = 1
PIECE = HERE // PIECES
CUT = NBD // PIECES


def padded(index, h):
    return pl.ds(1 + index * NBD + h * CUT, CUT)


def pieces(*refs):
    return [(t * PIECES + h, h, t, ref) for h in range(PIECES) for t, ref in enumerate(refs)]


def neighbours(x, y, z, c):
    pair = {"ctx": x * SIDE + y + 1 - 2 * lax.rem(y, 2)}
    other = {"head": 2 * z + 1 - c}
    up = {"head": 2 * lax.rem(z + 1, SIDE) + c}
    down = {"head": 2 * lax.rem(z + 3, SIDE) + c}
    return pair, other, up, down


def enter(senders, to_self):
    for device, mine in senders:
        if mine is None:
            greet(device)
        else:
            pl.when(jnp.logical_not(mine))(functools.partial(greet, device))
    pl.semaphore_wait(pltpu.get_barrier_semaphore(), len(senders) - to_self)


class Sends:
    def __init__(self):
        self.started, self.guarded = [], []

    def start(self, copy):
        copy.start()
        self.started.append(copy)

    def start_unless(self, mine, src, dst, send, recv, device):
        copy = remote(src, dst, send, recv, device)
        here = pltpu.make_async_copy(src, dst, recv)
        pl.when(jnp.logical_not(mine))(copy.start)
        pl.when(mine)(here.start)
        self.guarded.append((copy, mine))

    def wait(self):
        for copy in self.started:
            copy.wait_send()
        for copy, mine in self.guarded:
            pl.when(jnp.logical_not(mine))(copy.wait_send)


QUARTER = HERE // 4


def quarter(q):
    return pl.ds(q * QUARTER, QUARTER)


UNROLL = 10
MASKED = -1e30
NR = 4 * NBD * R
LAST = NR + G
LISTED = LAST + NB


def layer_kernel(
    aux, off, kvq, og, w, proj, dqh, dkh, dvh,
    ka, va, qa, doa, oa, dqa, probs, ogv, acc, dov, wv, dka, dva, dkg, dvg, runk, runv,
    oh, core_in, hop_in, z_in, stage, dcore, psend, nsend, dpair,
    ks, kr, qs, qr, ps, pr, fs, fr, ds, dr, zs, zr, cs, cr, own, wsem,
    os, orr, gs, gr, es, er, bs, br, hs, hr, c2s, c2r, as_, ar, z2s, z2r,
):
    ctx, hd, x, y, z, c = place()
    f32, bf16 = jnp.float32, jnp.bfloat16
    half = y // 2
    pair, other, up, down = neighbours(x, y, z, c)
    cw = lax.rem(half + c, 2)
    yw = query_row(y, cw)
    py = y + 1 - 2 * lax.rem(y, 2)
    near, pair_near = query_row(y, c), query_row(py, c)
    other_near, other_pair_near = query_row(y, 1 - c), query_row(py, 1 - c)
    to_self = 1 - jnp.minimum(c + half, 1)
    me = to_self == 1

    def worker(k):
        return {"ctx": k * SIDE + yw, "head": 2 * z + cw}

    senders = [
        ({"ctx": lax.rem(x + dx, SIDE) * SIDE + near, "head": 2 * z + half}, None if dx else me)
        for dx in range(SIDE)
    ]
    local = pltpu.make_async_copy(og, ogv.at[hd], own)
    local.start()
    weight = pltpu.make_async_copy(w, wv, wsem)
    weight.start()
    receivers = [
        ({"ctx": lax.rem(x + dx, SIDE) * SIDE + yw, "head": 2 * z + cw}, None if dx else me)
        for dx in range(SIDE)
    ]
    enter(senders + receivers + [(up, None), (down, None), (other, None), (pair, None)], 2 * to_self)

    sends, early = Sends(), Sends()

    def send_worker(src, dst, send, recv, dx, k):
        if dx:
            sends.start(remote(src, dst, send, recv, worker(k)))
        else:
            sends.start_unless(me, src, dst, send, recv, worker(k))

    def arrived(view, recv):
        remote(view, view, recv, recv, other).wait_recv()

    def send_pieces(dxs):
        for m, h, t, dst in pieces(ka, va):
            for dx in dxs:
                k = lax.rem(x + dx, SIDE)
                src = kvq.at[k, t, pl.ds(h * CUT, CUT)]
                send_worker(src, dst.at[padded(ctx, h)], ks.at[dx, m], kr.at[x, m], dx, k)

    send_pieces((0,))
    for q in range(4):
        for i, to, p in ((0, up, q), (1, down, (q + 2) % 4)):
            sends.start(remote(og.at[quarter(p)], ogv.at[hd, quarter(p)], zs.at[i, p], zr.at[i, p], to))
    send_pieces((1, 3))
    sends.start(remote(og, ogv.at[hd], cs.at[0], cr.at[0], other))
    dka[...] = jnp.zeros_like(dka)
    dva[...] = jnp.zeros_like(dva)
    for ref in (dkg, dvg):
        ref[...] = jnp.zeros_like(ref)
    for ref in (ka, va):
        ref[0] = jnp.zeros((BLOCK, HD), bf16)
        ref[NB + 1] = jnp.zeros((BLOCK, HD), bf16)
    for ref in (runk, runv):
        ref[0] = jnp.zeros((BLOCK, HD), f32)

    def add_shard(s):
        columns = pl.ds(pl.multiple_of(s * SHARD, SHARD), SHARD)

        def tile(i, carry):
            part = pl.ds(pl.multiple_of(i * PIECE, PIECE), PIECE)
            acc[part, :] += lax.dot_general(
                ogv[s, part, :], wv[:, columns], NT, preferred_element_type=f32
            )
            return carry

        lax.fori_loop(0, PIECES, tile, 0)

    def pass_near(dxs):
        for m, h, t, dst in pieces(ka, va):
            for dx in dxs:
                xs = lax.rem(x + SIDE - dx, SIDE)
                view = dst.at[padded(xs * SIDE + near, h)]
                arrived(view, kr.at[xs, m])
                sends.start(remote(view, view, ps.at[xs, m], pr.at[xs, m], pair))
                sends.start(remote(view, view, fs.at[xs, m], fr.at[xs, m], other))

    def pass_pair(dx):
        xs = lax.rem(x + SIDE - dx, SIDE)
        for m, h, t, dst in pieces(ka, va):
            view = dst.at[padded(xs * SIDE + pair_near, h)]
            arrived(view, pr.at[xs, m])
            sends.start(remote(view, view, fs.at[4 + xs, m], fr.at[4 + xs, m], other))

    below = 2 * lax.rem(z + 3, SIDE)
    above = 2 * lax.rem(z + 1, SIDE)
    across = 2 * lax.rem(z + 2, SIDE)

    pass_near((0,))
    for q in range(2):
        for i, s, to, p in ((0, below, up, q), (1, above, down, q + 2)):
            view = ogv.at[s + c, quarter(p)]
            arrived(view, zr.at[i, p])
            early.start(remote(view, view, zs.at[2, p], zr.at[2, p], to))
    pass_near((1, 3))
    send_pieces((2,))
    for dx in (0, 1, 3, 2):
        k = lax.rem(x + dx, SIDE)
        send_worker(kvq.at[k, 2], qa.at[blocks_of(x)], qs.at[dx], qr.at[x], dx, k)
    acc[...] = jnp.zeros_like(acc)
    local.wait()
    weight.wait()
    add_shard(hd)
    arrived(ogv.at[2 * z + 1 - c], cr.at[0])
    add_shard(2 * z + 1 - c)
    pass_near((2,))
    pass_pair(0)
    for i, s in ((0, below), (1, above)):
        for q in range(2):
            p = q + 2 - 2 * i
            arrived(ogv.at[s + c, quarter(p)], zr.at[i, p])
        early.start(remote(ogv.at[s + c], ogv.at[s + c], cs.at[1 + i], cr.at[1 + i], other))
        add_shard(s + c)
    for i, s in ((0, below), (1, above)):
        arrived(ogv.at[s + 1 - c], cr.at[1 + i])
        add_shard(s + 1 - c)
    pass_pair(1)
    for p in range(4):
        arrived(ogv.at[across + c, quarter(p)], zr.at[2, p])
    early.start(remote(ogv.at[across + c], ogv.at[across + c], cs.at[3], cr.at[3], other))
    add_shard(across + c)
    arrived(ogv.at[across + 1 - c], cr.at[3])
    add_shard(across + 1 - c)
    for k in range(HPD):
        dov[k] = acc[:, k * HD : (k + 1) * HD].astype(bf16).reshape(NBD, BLOCK, HD)
    for dx in (2, 1, 3, 0):
        k = lax.rem(x + dx, SIDE)
        send_worker(dov.at[k], doa.at[blocks_of(x)], ds.at[dx], dr.at[x], dx, k)
    pass_pair(3)
    pass_pair(2)
    for xs in range(SIDE):
        arrived(qa.at[blocks_of(xs)], qr.at[xs])
        for m, h, t, dst in pieces(ka, va):
            arrived(dst.at[padded(xs * SIDE + other_near, h)], fr.at[xs, m])
            arrived(dst.at[padded(xs * SIDE + other_pair_near, h)], fr.at[4 + xs, m])

    scale = 1.0 / math.sqrt(HD)

    def named(entry):
        return aux[LISTED + entry]

    g0, g1 = named(NR), named(NR + 1)
    column = lax.broadcasted_iota(jnp.int32, (1, 8 * BLOCK), 1) // BLOCK
    entry_is = [jnp.where(column == j, 1.0, 0.0).astype(f32) for j in range(8)]

    def listed(ref, window, randoms):
        near_rows = ref[window].reshape(3 * BLOCK, HD)
        return jnp.concatenate([near_rows, ref[g0], ref[g1]] + [ref[r] for r in randoms], axis=0)

    def work_of(turn, xs, m):
        for u in range(UNROLL):
            block = m * UNROLL + u
            n = turn * NBD + block
            i = (xs * SIDE + near) * NBD + block
            yield n, xs * NBD + block, i, pl.ds(i, 3), [named(n * R + r) for r in range(R)]

    def forward(turn, xs, m):
        work, biases = list(work_of(turn, xs, m)), []
        for n, _, i, _, _ in work:
            bias = entry_is[0] * jnp.where(i == 0, MASKED, 0.0) + entry_is[2] * jnp.where(i == NB - 1, MASKED, 0.0)
            for r in range(R):
                bias = bias + entry_is[5 + r] * off[n * R + r]
            biases.append(bias)
        kc = [listed(ka, t[3], t[4]) for t in work]
        vc = [listed(va, t[3], t[4]) for t in work]
        qn = [qa[t[1]] for t in work]
        s = [
            lax.dot_general(a, b, NT, preferred_element_type=f32) * scale + bias
            for a, b, bias in zip(qn, kc, biases)
        ]
        e = [jnp.exp(a - jnp.max(a, axis=1, keepdims=True)) for a in s]
        low_p = [(a * (1.0 / jnp.sum(a, axis=1, keepdims=True))).astype(bf16) for a in e]
        on = [jnp.dot(a, b, preferred_element_type=f32).astype(bf16) for a, b in zip(low_p, vc)]
        for t, a, b in zip(work, on, low_p):
            oa[t[1]] = a
            probs[t[1]] = b

    def backward(turn, xs, m):
        work = list(work_of(turn, xs, m))
        kc = [listed(ka, t[3], t[4]) for t in work]
        vc = [listed(va, t[3], t[4]) for t in work]
        qn = [qa[t[1]] for t in work]
        dn = [doa[t[1]] for t in work]
        low_p = [probs[t[1]] for t in work]
        dp = [lax.dot_general(a, b, NT, preferred_element_type=f32) for a, b in zip(dn, vc)]
        delta = [
            jnp.sum(a.astype(f32) * oa[t[1]].astype(f32), axis=1, keepdims=True) for a, t in zip(dn, work)
        ]
        dsc = [(a.astype(f32) * (b - d)).astype(bf16) for a, b, d in zip(low_p, dp, delta)]
        dvt = [lax.dot_general(a, b, TN, preferred_element_type=f32) for a, b in zip(low_p, dn)]
        dkt = [lax.dot_general(a, b, TN, preferred_element_type=f32) for a, b in zip(dsc, qn)]
        dqn = [
            (jnp.dot(a, b, preferred_element_type=f32) * scale).astype(bf16) for a, b in zip(dsc, kc)
        ]
        for t, a in zip(work, dqn):
            dqa[t[1]] = a
        for total, glob, run, terms in ((dka, dkg, runk, dkt), (dva, dvg, runv, dvt)):
            glob[...] += sum(a[3 * BLOCK : 5 * BLOCK] for a in terms).reshape(G, BLOCK, HD)
            for t, a in zip(work, terms):
                total[t[3]] += a[: 3 * BLOCK].reshape(3, BLOCK, HD)
                for r in range(R):
                    entry = t[0] * R + r
                    run[entry + 1] = a[(5 + r) * BLOCK : (6 + r) * BLOCK] + run[aux[entry]]

    def home_of(xs):
        return {"ctx": xs * SIDE + near, "head": 2 * z + half}

    def source_turn(turn, carry):
        xs = lax.rem(x + turn + 1, SIDE)

        def half_turn(m, inner):
            forward(turn, xs, m)
            return inner

        lax.fori_loop(0, NBD // UNROLL, half_turn, 0)
        mine = me & (turn == SIDE - 1)
        copy = remote(oa.at[blocks_of(xs)], oh.at[x], os.at[turn], orr.at[x], home_of(xs))
        here = pltpu.make_async_copy(oa.at[blocks_of(xs)], oh.at[x], orr.at[x])
        pl.when(jnp.logical_not(mine))(copy.start)
        pl.when(mine)(here.start)
        return carry

    lax.fori_loop(0, SIDE, source_turn, 0)
    for xs in range(SIDE):
        arrived(doa.at[blocks_of(xs)], dr.at[xs])

    def back_turn(turn, carry):
        xs = lax.rem(x + turn + 1, SIDE)

        def half_turn(m, inner):
            backward(turn, xs, m)
            return inner

        lax.fori_loop(0, NBD // UNROLL, half_turn, 0)
        return carry

    lax.fori_loop(0, SIDE, back_turn, 0)
    for i in range(SIDE):
        xs = lax.rem(x + i + 1, SIDE)
        copy = remote(oa.at[blocks_of(xs)], oh.at[x], os.at[i], orr.at[x], home_of(xs))
        if i < SIDE - 1:
            sends.started.append(copy)
        else:
            sends.guarded.append((copy, me))
    for run, glob in ((runk, dkg), (runv, dvg)):
        for i in range(G):
            run[NR + i + 1] = glob[i] + run[aux[NR + i]]
    early.wait()

    def put_sum(ref, j, t, h, total, run, index, factor, also):
        def block(n, carry):
            here = h * CUT + n
            u = index * NBD + here
            value = (total[u + 1] + run[aux[LAST + u]]) * factor
            for other_ref, slot in also:
                value = value + other_ref[slot, t, here].astype(f32)
            ref[j, t, here] = value.astype(bf16)
            return carry

        lax.fori_loop(0, CUT, block, 0)

    totals = ((dka, runk, scale), (dva, runv, 1.0))

    def part(h):
        return pl.ds(h * CUT, CUT)

    def for_other_core(g, there, dx):
        xs = lax.rem(x + dx, SIDE)
        for m, h, t, (total, run, factor) in pieces(*totals):
            put_sum(stage, g + xs, t, h, total, run, xs * SIDE + there, factor, ())
            sends.start(
                remote(stage.at[g + xs, t, part(h)], dcore.at[g + xs, t, part(h)], es.at[g + xs, m], er.at[g + xs, m], other)
            )

    def for_pair(dx):
        xs = lax.rem(x + dx, SIDE)
        for m, h, t, (total, run, factor) in pieces(*totals):
            arrived(dcore.at[xs, t, part(h)], er.at[xs, m])
            put_sum(psend, xs, t, h, total, run, xs * SIDE + pair_near, factor, ((dcore, xs),))
            sends.start(
                remote(psend.at[xs, t, part(h)], dpair.at[xs, t, part(h)], bs.at[xs, m], br.at[xs, m], pair)
            )

    def finish(dx):
        xs = lax.rem(x + dx, SIDE)
        for m, h, t, (total, run, factor) in pieces(*totals):
            arrived(dcore.at[4 + xs, t, part(h)], er.at[4 + xs, m])
            arrived(dpair.at[xs, t, part(h)], br.at[xs, m])
            put_sum(
                nsend, xs, t, h, total, run, xs * SIDE + near, factor, ((dcore, 4 + xs), (dpair, xs))
            )
            src, dst = nsend.at[xs, t, part(h)], (dkh, dvh)[t].at[x, part(h)]
            if dx:
                sends.start(remote(src, dst, hs.at[dx, m], hr.at[x, m], home_of(xs)))
            else:
                sends.start_unless(me, src, dst, hs.at[dx, m], hr.at[x, m], home_of(xs))

    for dx in (2, 1, 3, 0):
        for_other_core(0, other_pair_near, dx)
    for_pair(2)
    for_pair(1)
    for k in range(HPD):
        arrived(oh.at[k], orr.at[k])
    for i in range(SIDE):
        xs = lax.rem(x + i + 1, SIDE)
        args = dqa.at[blocks_of(xs)], dqh.at[x], gs.at[i], gr.at[x], home_of(xs)
        if i < SIDE - 1:
            sends.start(remote(*args))
        else:
            sends.start_unless(me, *args)

    def shard_product(s, put):
        columns = pl.ds(pl.multiple_of(s * SHARD, SHARD), SHARD)

        def tile(i, carry):
            rows = pl.ds(pl.multiple_of(i * PIECE, PIECE), PIECE)
            left = [oh[k, pl.ds(i * CUT, CUT)].reshape(PIECE, HD) for k in range(HPD)]
            left = jnp.concatenate(left, axis=1)
            put(rows, jnp.dot(left, wv[:, columns], preferred_element_type=f32))
            return carry

        lax.fori_loop(0, PIECES, tile, 0)

    for i, s in enumerate((across, above, below, 2 * z)):

        def put(rows, value):
            ogv[i, rows, :] = value.astype(bf16)

        shard_product(s + 1 - c, put)
        sends.start(remote(ogv.at[i], core_in.at[i], c2s.at[i], c2r.at[i], other))

    arrived(core_in.at[0], c2r.at[0])

    def put_across(rows, value):
        ogv[4, rows, :] = (value + core_in[0, rows, :].astype(f32)).astype(bf16)

    shard_product(across + c, put_across)
    for q in range(4):
        sends.start(
            remote(
                ogv.at[4, quarter(q)], hop_in.at[quarter(q)], as_.at[q], ar.at[q], up if q < 2 else down
            )
        )
    for i, s, to in ((0, above, up), (1, below, down)):
        arrived(core_in.at[1 + i], c2r.at[1 + i])

        def put_near(rows, value):
            ogv[5 + i, rows, :] = (value + core_in[1 + i, rows, :].astype(f32)).astype(bf16)

        shard_product(s + c, put_near)
        for q in (2 - 2 * i, 3 - 2 * i):
            sends.start(
                remote(ogv.at[5 + i, quarter(q)], z_in.at[i, quarter(q)], z2s.at[i, q], z2r.at[i, q], to)
            )
    arrived(core_in.at[3], c2r.at[3])

    def put_own(rows, value):
        acc[rows, :] = value + core_in[3, rows, :].astype(f32)

    for_pair(3)
    for_pair(0)
    for dx in (2, 1, 3, 0):
        for_other_core(4, other_near, dx)
    shard_product(hd, put_own)
    for q in range(2):
        for i, to in ((0, up), (1, down)):
            p = q + 2 * i
            arrived(hop_in.at[quarter(p)], ar.at[p])
            ogv[5 + i, quarter(p), :] = (
                ogv[5 + i, quarter(p), :].astype(f32) + hop_in[quarter(p), :].astype(f32)
            ).astype(bf16)
            sends.start(
                remote(ogv.at[5 + i, quarter(p)], z_in.at[i, quarter(p)], z2s.at[i, p], z2r.at[i, p], to)
            )
    for dx in (2, 1, 3, 0):
        finish(dx)
    for i in range(2):
        for q in range(4):
            arrived(z_in.at[i, quarter(q)], z2r.at[i, q])
    proj[...] = (acc[...] + z_in[0].astype(f32) + z_in[1].astype(f32)).astype(bf16)
    for k in range(HPD):
        arrived(dqh.at[k], gr.at[k])
        for m, h, t, out in pieces(dkh, dvh):
            arrived(out.at[k, part(h)], hr.at[k, m])
    sends.wait()


ANY = pl.BlockSpec(memory_space=pl.ANY)
VMEM = pl.BlockSpec(memory_space=pltpu.VMEM)
SMEM = pl.BlockSpec(memory_space=pltpu.SMEM)
LIMIT = 60 * 1024 * 1024


def struct(*shape):
    return jax.ShapeDtypeStruct(shape, jnp.bfloat16)


def sem(*shape):
    return pltpu.SemaphoreType.DMA(shape)


def prepare_kernel(rid, cnt, gid, k, v, q, kvq, aux, off):
    _, _, x, y, _, c = place()
    near = query_row(y, c)

    def clear(b, carry):
        aux[LAST + b] = 0
        return carry

    lax.fori_loop(0, NB, clear, 0, unroll=32)

    def enter_block(entry, block):
        aux[entry] = aux[LAST + block]
        aux[LAST + block] = entry + 1
        aux[LISTED + entry] = block + 1

    for turn in range(SIDE):
        first = (lax.rem(x + turn + 1, SIDE) * SIDE + near) * NBD

        def query_block(b, carry):
            i = first + b
            for r in range(R):
                entry = (turn * NBD + b) * R + r
                enter_block(entry, rid[r, i])
                off[entry] = jnp.where(r < cnt[i], 0.0, MASKED).astype(jnp.float32)
            if turn < 3:
                rows = (k, v, q)[turn][pl.ds(b * BLOCK, BLOCK)]
                kvq[:, turn, b] = jnp.swapaxes(rows, 0, 1)
            return carry

        lax.fori_loop(0, NBD, query_block, 0, unroll=5)
    for g in range(G):
        enter_block(NR + g, gid[g])


def finish_kernel(dqh, dkh, dvh, summed, dq, dk, dv, projected):
    projected[...] = summed[...]
    for ref, out in ((dqh, dq), (dkh, dk), (dvh, dv)):
        out[...] = jnp.swapaxes(ref[...].reshape(HPD, HERE, HD), 0, 1)


def local(queries, key_rows, value_rows, out_weight, out_grad, global_ids, random_ids, random_count):
    bf16, f32 = jnp.bfloat16, jnp.float32
    kvq, aux, off = pl.pallas_call(
        prepare_kernel,
        out_shape=(
            struct(HPD, 3, NBD, BLOCK, HD),
            jax.ShapeDtypeStruct((LISTED + NR + G,), jnp.int32),
            jax.ShapeDtypeStruct((NR,), jnp.float32),
        ),
        in_specs=[SMEM] * 3 + [VMEM] * 3,
        out_specs=(VMEM, SMEM, SMEM),
        compiler_params=pltpu.CompilerParams(vmem_limit_bytes=LIMIT),
    )(random_ids.T, random_count, global_ids, key_rows, value_rows, queries)
    w = out_weight.reshape(HPD * HD, out_weight.shape[2])
    both = 2 * PIECES

    def vmem(*shape, dtype=bf16):
        return pltpu.VMEM(shape, dtype)

    def blocks(*count, dtype=bf16):
        return vmem(*count, BLOCK, HD, dtype=dtype)

    one = pltpu.SemaphoreType.DMA
    summed, dqh, dkh, dvh = pl.pallas_call(
        layer_kernel,
        out_shape=(struct(HERE, SHARD),) + (struct(HPD, NBD, BLOCK, HD),) * 3,
        in_specs=[SMEM, SMEM, ANY, ANY, ANY],
        out_specs=(VMEM, ANY, ANY, ANY),
        scratch_shapes=[
            blocks(NB + 2), blocks(NB + 2), blocks(4 * NBD), blocks(4 * NBD), blocks(4 * NBD), blocks(4 * NBD),
            vmem(4 * NBD, BLOCK, 8 * BLOCK),
            vmem(8, HERE, SHARD), vmem(HERE, SHARD, dtype=f32), blocks(HPD, NBD), vmem(*w.shape),
            blocks(NB + 2, dtype=f32), blocks(NB + 2, dtype=f32), blocks(G, dtype=f32), blocks(G, dtype=f32),
            blocks(NR + G + 1, dtype=f32), blocks(NR + G + 1, dtype=f32),
            blocks(HPD, NBD), vmem(4, HERE, SHARD), vmem(HERE, SHARD), vmem(2, HERE, SHARD),
            blocks(8, 2, NBD), blocks(8, 2, NBD), blocks(4, 2, NBD), blocks(4, 2, NBD), blocks(4, 2, NBD),
            sem(4, both), sem(4, both), sem(4), sem(4), sem(4, both), sem(4, both), sem(8, both), sem(8, both),
            sem(4), sem(4), sem(3, 4), sem(3, 4), sem(4), sem(4), one, one,
            sem(4), sem(4), sem(4), sem(4), sem(8, both), sem(8, both), sem(4, both), sem(4, both),
            sem(4, both), sem(4, both), sem(4), sem(4), sem(4), sem(4), sem(2, 4), sem(2, 4),
        ],
        compiler_params=pltpu.CompilerParams(
            collective_id=0, has_side_effects=True, vmem_limit_bytes=LIMIT
        ),
    )(aux, off, kvq, out_grad, w)
    *grads, projected = pl.pallas_call(
        finish_kernel,
        out_shape=(struct(HERE, HPD, HD),) * 3 + (struct(HERE, SHARD),),
        in_specs=[VMEM] * 4,
        out_specs=(VMEM,) * 4,
        compiler_params=pltpu.CompilerParams(vmem_limit_bytes=LIMIT),
    )(dqh, dkh, dvh, summed)
    return (projected, *grads)


def solution(mesh):
    placed = (
        P("ctx", "head", None),
        P("ctx", "head", None),
        P("ctx", "head", None),
        P("head", None, None),
        P("ctx", "head"),
        P(),
        P(),
        P(),
    )
    return jax.shard_map(
        local,
        mesh=mesh,
        in_specs=placed,
        out_specs=(
            P("ctx", "head"),
            P("ctx", "head", None),
            P("ctx", "head", None),
            P("ctx", "head", None),
        ),
        check_vma=False,
    )
```

```python
import functools
import math

import jax
import jax.numpy as jnp
from jax import lax
from jax.experimental import pallas as pl
from jax.experimental.pallas import tpu as pltpu
from jax.sharding import PartitionSpec as P

SIDE = 4
BLOCK = 64
G = 2
R = 3
HERE = 640
NBD = 10
HD = 128
HPD = 4
NB = 160
SHARD = 512
MESH = pl.DeviceIdType.MESH
NT = (((1,), (1,)), ((), ()))
TN = (((0,), (0,)), ((), ()))


def place():
    ctx, hd = lax.axis_index("ctx"), lax.axis_index("head")
    return ctx, hd, ctx // SIDE, lax.rem(ctx, SIDE), hd // 2, lax.rem(hd, 2)


def query_row(y, c):
    return y * (1 - c) + (3 - y) * c


def remote(src, dst, send, recv, device):
    return pltpu.make_async_remote_copy(
        src_ref=src, dst_ref=dst, send_sem=send, recv_sem=recv, device_id=device, device_id_type=MESH
    )


def greet(device):
    pl.semaphore_signal(pltpu.get_barrier_semaphore(), inc=1, device_id=device, device_id_type=MESH)


def blocks_of(index):
    return pl.ds(index * NBD, NBD)


PIECES = 1
PIECE = HERE // PIECES
CUT = NBD // PIECES


def padded(index, h):
    return pl.ds(1 + index * NBD + h * CUT, CUT)


def pieces(*refs):
    return [(t * PIECES + h, h, t, ref) for h in range(PIECES) for t, ref in enumerate(refs)]


def neighbours(x, y, z, c):
    pair = {"ctx": x * SIDE + y + 1 - 2 * lax.rem(y, 2)}
    other = {"head": 2 * z + 1 - c}
    up = {"head": 2 * lax.rem(z + 1, SIDE) + c}
    down = {"head": 2 * lax.rem(z + 3, SIDE) + c}
    return pair, other, up, down


def enter(senders, to_self):
    for device, mine in senders:
        if mine is None:
            greet(device)
        else:
            pl.when(jnp.logical_not(mine))(functools.partial(greet, device))
    pl.semaphore_wait(pltpu.get_barrier_semaphore(), len(senders) - to_self)


class Sends:
    def __init__(self):
        self.started, self.guarded = [], []

    def start(self, copy):
        copy.start()
        self.started.append(copy)

    def start_unless(self, mine, src, dst, send, recv, device):
        copy = remote(src, dst, send, recv, device)
        here = pltpu.make_async_copy(src, dst, recv)
        pl.when(jnp.logical_not(mine))(copy.start)
        pl.when(mine)(here.start)
        self.guarded.append((copy, mine))

    def wait(self):
        for copy in self.started:
            copy.wait_send()
        for copy, mine in self.guarded:
            pl.when(jnp.logical_not(mine))(copy.wait_send)


QUARTER = HERE // 4


def quarter(q):
    return pl.ds(q * QUARTER, QUARTER)


UNROLL = 10
MASKED = -1e30
NR = 4 * NBD * R
LAST = NR + G
LISTED = LAST + NB


def layer_kernel(
    aux, off, kvq, og, w, proj, dqh, dkh, dvh,
    ka, va, qa, doa, oa, dqa, probs, ogv, acc, dov, wv, dka, dva, dkg, dvg, runk, runv,
    oh, core_in, hop_in, z_in, stage, dcore, psend, nsend, dpair,
    ks, kr, qs, qr, ps, pr, fs, fr, ds, dr, zs, zr, cs, cr, own, wsem,
    os, orr, gs, gr, es, er, bs, br, hs, hr, c2s, c2r, as_, ar, z2s, z2r,
):
    ctx, hd, x, y, z, c = place()
    f32, bf16 = jnp.float32, jnp.bfloat16
    half = y // 2
    pair, other, up, down = neighbours(x, y, z, c)
    cw = lax.rem(half + c, 2)
    yw = query_row(y, cw)
    py = y + 1 - 2 * lax.rem(y, 2)
    near, pair_near = query_row(y, c), query_row(py, c)
    other_near, other_pair_near = query_row(y, 1 - c), query_row(py, 1 - c)
    to_self = 1 - jnp.minimum(c + half, 1)
    me = to_self == 1

    def worker(k):
        return {"ctx": k * SIDE + yw, "head": 2 * z + cw}

    senders = [
        ({"ctx": lax.rem(x + dx, SIDE) * SIDE + near, "head": 2 * z + half}, None if dx else me)
        for dx in range(SIDE)
    ]
    local = pltpu.make_async_copy(og, ogv.at[hd], own)
    local.start()
    weight = pltpu.make_async_copy(w, wv, wsem)
    weight.start()
    receivers = [
        ({"ctx": lax.rem(x + dx, SIDE) * SIDE + yw, "head": 2 * z + cw}, None if dx else me)
        for dx in range(SIDE)
    ]
    enter(senders + receivers + [(up, None), (down, None), (other, None), (pair, None)], 2 * to_self)

    sends, early = Sends(), Sends()

    def send_worker(src, dst, send, recv, dx, k):
        if dx:
            sends.start(remote(src, dst, send, recv, worker(k)))
        else:
            sends.start_unless(me, src, dst, send, recv, worker(k))

    def arrived(view, recv):
        remote(view, view, recv, recv, other).wait_recv()

    def send_pieces(dxs):
        for m, h, t, dst in pieces(ka, va):
            for dx in dxs:
                k = lax.rem(x + dx, SIDE)
                src = kvq.at[k, t, pl.ds(h * CUT, CUT)]
                send_worker(src, dst.at[padded(ctx, h)], ks.at[dx, m], kr.at[x, m], dx, k)

    send_pieces((0,))
    for q in range(4):
        for i, to, p in ((0, up, q), (1, down, (q + 2) % 4)):
            sends.start(remote(og.at[quarter(p)], ogv.at[hd, quarter(p)], zs.at[i, p], zr.at[i, p], to))
    send_pieces((1, 3))
    sends.start(remote(og, ogv.at[hd], cs.at[0], cr.at[0], other))
    dka[...] = jnp.zeros_like(dka)
    dva[...] = jnp.zeros_like(dva)
    for ref in (dkg, dvg):
        ref[...] = jnp.zeros_like(ref)
    for ref in (ka, va):
        ref[0] = jnp.zeros((BLOCK, HD), bf16)
        ref[NB + 1] = jnp.zeros((BLOCK, HD), bf16)
    for ref in (runk, runv):
        ref[0] = jnp.zeros((BLOCK, HD), f32)

    def add_shard(s):
        columns = pl.ds(pl.multiple_of(s * SHARD, SHARD), SHARD)

        def tile(i, carry):
            part = pl.ds(pl.multiple_of(i * PIECE, PIECE), PIECE)
            acc[part, :] += lax.dot_general(
                ogv[s, part, :], wv[:, columns], NT, preferred_element_type=f32
            )
            return carry

        lax.fori_loop(0, PIECES, tile, 0)

    def pass_near(dxs):
        for m, h, t, dst in pieces(ka, va):
            for dx in dxs:
                xs = lax.rem(x + SIDE - dx, SIDE)
                view = dst.at[padded(xs * SIDE + near, h)]
                arrived(view, kr.at[xs, m])
                sends.start(remote(view, view, ps.at[xs, m], pr.at[xs, m], pair))
                sends.start(remote(view, view, fs.at[xs, m], fr.at[xs, m], other))

    def pass_pair(dx):
        xs = lax.rem(x + SIDE - dx, SIDE)
        for m, h, t, dst in pieces(ka, va):
            view = dst.at[padded(xs * SIDE + pair_near, h)]
            arrived(view, pr.at[xs, m])
            sends.start(remote(view, view, fs.at[4 + xs, m], fr.at[4 + xs, m], other))

    below = 2 * lax.rem(z + 3, SIDE)
    above = 2 * lax.rem(z + 1, SIDE)
    across = 2 * lax.rem(z + 2, SIDE)

    pass_near((0,))
    for q in range(2):
        for i, s, to, p in ((0, below, up, q), (1, above, down, q + 2)):
            view = ogv.at[s + c, quarter(p)]
            arrived(view, zr.at[i, p])
            early.start(remote(view, view, zs.at[2, p], zr.at[2, p], to))
    pass_near((1, 3))
    send_pieces((2,))
    for dx in (0, 1, 3, 2):
        k = lax.rem(x + dx, SIDE)
        send_worker(kvq.at[k, 2], qa.at[blocks_of(x)], qs.at[dx], qr.at[x], dx, k)
    acc[...] = jnp.zeros_like(acc)
    local.wait()
    weight.wait()
    add_shard(hd)
    arrived(ogv.at[2 * z + 1 - c], cr.at[0])
    add_shard(2 * z + 1 - c)
    pass_near((2,))
    for i, s in ((0, below), (1, above)):
        for q in range(2):
            p = q + 2 - 2 * i
            arrived(ogv.at[s + c, quarter(p)], zr.at[i, p])
        early.start(remote(ogv.at[s + c], ogv.at[s + c], cs.at[1 + i], cr.at[1 + i], other))
        add_shard(s + c)
    for p in range(4):
        arrived(ogv.at[across + c, quarter(p)], zr.at[2, p])
    early.start(remote(ogv.at[across + c], ogv.at[across + c], cs.at[3], cr.at[3], other))
    for i, s in ((0, below), (1, above)):
        arrived(ogv.at[s + 1 - c], cr.at[1 + i])
        add_shard(s + 1 - c)
    add_shard(across + c)
    arrived(ogv.at[across + 1 - c], cr.at[3])
    add_shard(across + 1 - c)
    for k in range(HPD):
        dov[k] = acc[:, k * HD : (k + 1) * HD].astype(bf16).reshape(NBD, BLOCK, HD)
    for dx in (2, 1, 3, 0):
        k = lax.rem(x + dx, SIDE)
        send_worker(dov.at[k], doa.at[blocks_of(x)], ds.at[dx], dr.at[x], dx, k)
    pass_pair(0)
    pass_pair(1)
    pass_pair(3)
    pass_pair(2)
    for xs in range(SIDE):
        arrived(qa.at[blocks_of(xs)], qr.at[xs])
        for m, h, t, dst in pieces(ka, va):
            arrived(dst.at[padded(xs * SIDE + other_near, h)], fr.at[xs, m])
            arrived(dst.at[padded(xs * SIDE + other_pair_near, h)], fr.at[4 + xs, m])

    scale = 1.0 / math.sqrt(HD)

    def named(entry):
        return aux[LISTED + entry]

    g0, g1 = named(NR), named(NR + 1)
    column = lax.broadcasted_iota(jnp.int32, (1, 8 * BLOCK), 1) // BLOCK
    entry_is = [jnp.where(column == j, 1.0, 0.0).astype(f32) for j in range(8)]

    def listed(ref, window, randoms):
        near_rows = ref[window].reshape(3 * BLOCK, HD)
        return jnp.concatenate([near_rows, ref[g0], ref[g1]] + [ref[r] for r in randoms], axis=0)

    def work_of(turn, xs, m):
        for u in range(UNROLL):
            block = m * UNROLL + u
            n = turn * NBD + block
            i = (xs * SIDE + near) * NBD + block
            yield n, xs * NBD + block, i, pl.ds(i, 3), [named(n * R + r) for r in range(R)]

    def forward(turn, xs, m):
        work, biases = list(work_of(turn, xs, m)), []
        for n, _, i, _, _ in work:
            bias = entry_is[0] * jnp.where(i == 0, MASKED, 0.0) + entry_is[2] * jnp.where(i == NB - 1, MASKED, 0.0)
            for r in range(R):
                bias = bias + entry_is[5 + r] * off[n * R + r]
            biases.append(bias)
        kc = [listed(ka, t[3], t[4]) for t in work]
        vc = [listed(va, t[3], t[4]) for t in work]
        qn = [qa[t[1]] for t in work]
        s = [
            lax.dot_general(a, b, NT, preferred_element_type=f32) * scale + bias
            for a, b, bias in zip(qn, kc, biases)
        ]
        e = [jnp.exp(a - jnp.max(a, axis=1, keepdims=True)) for a in s]
        low_p = [(a * (1.0 / jnp.sum(a, axis=1, keepdims=True))).astype(bf16) for a in e]
        on = [jnp.dot(a, b, preferred_element_type=f32).astype(bf16) for a, b in zip(low_p, vc)]
        for t, a, b in zip(work, on, low_p):
            oa[t[1]] = a
            probs[t[1]] = b

    def backward(turn, xs, m):
        work = list(work_of(turn, xs, m))
        kc = [listed(ka, t[3], t[4]) for t in work]
        vc = [listed(va, t[3], t[4]) for t in work]
        qn = [qa[t[1]] for t in work]
        dn = [doa[t[1]] for t in work]
        low_p = [probs[t[1]] for t in work]
        dp = [lax.dot_general(a, b, NT, preferred_element_type=f32) for a, b in zip(dn, vc)]
        delta = [
            jnp.sum(a.astype(f32) * oa[t[1]].astype(f32), axis=1, keepdims=True) for a, t in zip(dn, work)
        ]
        dsc = [(a.astype(f32) * (b - d)).astype(bf16) for a, b, d in zip(low_p, dp, delta)]
        dvt = [lax.dot_general(a, b, TN, preferred_element_type=f32) for a, b in zip(low_p, dn)]
        dkt = [lax.dot_general(a, b, TN, preferred_element_type=f32) for a, b in zip(dsc, qn)]
        dqn = [
            (jnp.dot(a, b, preferred_element_type=f32) * scale).astype(bf16) for a, b in zip(dsc, kc)
        ]
        for t, a in zip(work, dqn):
            dqa[t[1]] = a
        for total, glob, run, terms in ((dka, dkg, runk, dkt), (dva, dvg, runv, dvt)):
            glob[...] += sum(a[3 * BLOCK : 5 * BLOCK] for a in terms).reshape(G, BLOCK, HD)
            for t, a in zip(work, terms):
                total[t[3]] += a[: 3 * BLOCK].reshape(3, BLOCK, HD)
                for r in range(R):
                    entry = t[0] * R + r
                    run[entry + 1] = a[(5 + r) * BLOCK : (6 + r) * BLOCK] + run[aux[entry]]

    def home_of(xs):
        return {"ctx": xs * SIDE + near, "head": 2 * z + half}

    def source_turn(turn, carry):
        xs = lax.rem(x + turn + 1, SIDE)

        def half_turn(m, inner):
            forward(turn, xs, m)
            return inner

        lax.fori_loop(0, NBD // UNROLL, half_turn, 0)
        mine = me & (turn == SIDE - 1)
        copy = remote(oa.at[blocks_of(xs)], oh.at[x], os.at[turn], orr.at[x], home_of(xs))
        here = pltpu.make_async_copy(oa.at[blocks_of(xs)], oh.at[x], orr.at[x])
        pl.when(jnp.logical_not(mine))(copy.start)
        pl.when(mine)(here.start)
        return carry

    lax.fori_loop(0, SIDE, source_turn, 0)
    for xs in range(SIDE):
        arrived(doa.at[blocks_of(xs)], dr.at[xs])

    def back_turn(turn, carry):
        xs = lax.rem(x + turn + 1, SIDE)

        def half_turn(m, inner):
            backward(turn, xs, m)
            return inner

        lax.fori_loop(0, NBD // UNROLL, half_turn, 0)
        return carry

    lax.fori_loop(0, SIDE, back_turn, 0)
    for i in range(SIDE):
        xs = lax.rem(x + i + 1, SIDE)
        copy = remote(oa.at[blocks_of(xs)], oh.at[x], os.at[i], orr.at[x], home_of(xs))
        if i < SIDE - 1:
            sends.started.append(copy)
        else:
            sends.guarded.append((copy, me))
    for run, glob in ((runk, dkg), (runv, dvg)):
        for i in range(G):
            run[NR + i + 1] = glob[i] + run[aux[NR + i]]
    early.wait()

    def put_sum(ref, j, t, h, total, run, index, factor, also):
        def block(n, carry):
            here = h * CUT + n
            u = index * NBD + here
            value = (total[u + 1] + run[aux[LAST + u]]) * factor
            for other_ref, slot in also:
                value = value + other_ref[slot, t, here].astype(f32)
            ref[j, t, here] = value.astype(bf16)
            return carry

        lax.fori_loop(0, CUT, block, 0)

    totals = ((dka, runk, scale), (dva, runv, 1.0))

    def part(h):
        return pl.ds(h * CUT, CUT)

    def for_other_core(g, there, dx):
        xs = lax.rem(x + dx, SIDE)
        for m, h, t, (total, run, factor) in pieces(*totals):
            put_sum(stage, g + xs, t, h, total, run, xs * SIDE + there, factor, ())
            sends.start(
                remote(stage.at[g + xs, t, part(h)], dcore.at[g + xs, t, part(h)], es.at[g + xs, m], er.at[g + xs, m], other)
            )

    def for_pair(dx):
        xs = lax.rem(x + dx, SIDE)
        for m, h, t, (total, run, factor) in pieces(*totals):
            arrived(dcore.at[xs, t, part(h)], er.at[xs, m])
            put_sum(psend, xs, t, h, total, run, xs * SIDE + pair_near, factor, ((dcore, xs),))
            sends.start(
                remote(psend.at[xs, t, part(h)], dpair.at[xs, t, part(h)], bs.at[xs, m], br.at[xs, m], pair)
            )

    def finish(dx):
        xs = lax.rem(x + dx, SIDE)
        for m, h, t, (total, run, factor) in pieces(*totals):
            arrived(dcore.at[4 + xs, t, part(h)], er.at[4 + xs, m])
            arrived(dpair.at[xs, t, part(h)], br.at[xs, m])
            put_sum(
                nsend, xs, t, h, total, run, xs * SIDE + near, factor, ((dcore, 4 + xs), (dpair, xs))
            )
            src, dst = nsend.at[xs, t, part(h)], (dkh, dvh)[t].at[x, part(h)]
            if dx:
                sends.start(remote(src, dst, hs.at[dx, m], hr.at[x, m], home_of(xs)))
            else:
                sends.start_unless(me, src, dst, hs.at[dx, m], hr.at[x, m], home_of(xs))

    for dx in (2, 1, 3, 0):
        for_other_core(0, other_pair_near, dx)
    for_pair(2)
    for_pair(1)
    for k in range(HPD):
        arrived(oh.at[k], orr.at[k])
    for i in range(SIDE):
        xs = lax.rem(x + i + 1, SIDE)
        args = dqa.at[blocks_of(xs)], dqh.at[x], gs.at[i], gr.at[x], home_of(xs)
        if i < SIDE - 1:
            sends.start(remote(*args))
        else:
            sends.start_unless(me, *args)

    def shard_product(s, put):
        columns = pl.ds(pl.multiple_of(s * SHARD, SHARD), SHARD)

        def tile(i, carry):
            rows = pl.ds(pl.multiple_of(i * PIECE, PIECE), PIECE)
            left = [oh[k, pl.ds(i * CUT, CUT)].reshape(PIECE, HD) for k in range(HPD)]
            left = jnp.concatenate(left, axis=1)
            put(rows, jnp.dot(left, wv[:, columns], preferred_element_type=f32))
            return carry

        lax.fori_loop(0, PIECES, tile, 0)

    for i, s in enumerate((across, above, below, 2 * z)):

        def put(rows, value):
            ogv[i, rows, :] = value.astype(bf16)

        shard_product(s + 1 - c, put)
        sends.start(remote(ogv.at[i], core_in.at[i], c2s.at[i], c2r.at[i], other))

    arrived(core_in.at[0], c2r.at[0])

    def put_across(rows, value):
        ogv[4, rows, :] = (value + core_in[0, rows, :].astype(f32)).astype(bf16)

    shard_product(across + c, put_across)
    for q in range(4):
        sends.start(
            remote(
                ogv.at[4, quarter(q)], hop_in.at[quarter(q)], as_.at[q], ar.at[q], up if q < 2 else down
            )
        )
    for i, s, to in ((0, above, up), (1, below, down)):
        arrived(core_in.at[1 + i], c2r.at[1 + i])

        def put_near(rows, value):
            ogv[5 + i, rows, :] = (value + core_in[1 + i, rows, :].astype(f32)).astype(bf16)

        shard_product(s + c, put_near)
        for q in (2 - 2 * i, 3 - 2 * i):
            sends.start(
                remote(ogv.at[5 + i, quarter(q)], z_in.at[i, quarter(q)], z2s.at[i, q], z2r.at[i, q], to)
            )
    arrived(core_in.at[3], c2r.at[3])

    def put_own(rows, value):
        acc[rows, :] = value + core_in[3, rows, :].astype(f32)

    for_pair(3)
    for_pair(0)
    for dx in (2, 1, 3, 0):
        for_other_core(4, other_near, dx)
    shard_product(hd, put_own)
    for q in range(2):
        for i, to in ((0, up), (1, down)):
            p = q + 2 * i
            arrived(hop_in.at[quarter(p)], ar.at[p])
            ogv[5 + i, quarter(p), :] = (
                ogv[5 + i, quarter(p), :].astype(f32) + hop_in[quarter(p), :].astype(f32)
            ).astype(bf16)
            sends.start(
                remote(ogv.at[5 + i, quarter(p)], z_in.at[i, quarter(p)], z2s.at[i, p], z2r.at[i, p], to)
            )
    for dx in (2, 1, 3, 0):
        finish(dx)
    for i in range(2):
        for q in range(4):
            arrived(z_in.at[i, quarter(q)], z2r.at[i, q])
    proj[...] = (acc[...] + z_in[0].astype(f32) + z_in[1].astype(f32)).astype(bf16)
    for k in range(HPD):
        arrived(dqh.at[k], gr.at[k])
        for m, h, t, out in pieces(dkh, dvh):
            arrived(out.at[k, part(h)], hr.at[k, m])
    sends.wait()


ANY = pl.BlockSpec(memory_space=pl.ANY)
VMEM = pl.BlockSpec(memory_space=pltpu.VMEM)
SMEM = pl.BlockSpec(memory_space=pltpu.SMEM)
LIMIT = 60 * 1024 * 1024


def struct(*shape):
    return jax.ShapeDtypeStruct(shape, jnp.bfloat16)


def sem(*shape):
    return pltpu.SemaphoreType.DMA(shape)


def prepare_kernel(rid, cnt, gid, k, v, q, kvq, aux, off):
    _, _, x, y, _, c = place()
    near = query_row(y, c)

    def clear(b, carry):
        aux[LAST + b] = 0
        return carry

    lax.fori_loop(0, NB, clear, 0, unroll=32)

    def enter_block(entry, block):
        aux[entry] = aux[LAST + block]
        aux[LAST + block] = entry + 1
        aux[LISTED + entry] = block + 1

    for turn in range(SIDE):
        first = (lax.rem(x + turn + 1, SIDE) * SIDE + near) * NBD

        def query_block(b, carry):
            i = first + b
            for r in range(R):
                entry = (turn * NBD + b) * R + r
                enter_block(entry, rid[r, i])
                off[entry] = jnp.where(r < cnt[i], 0.0, MASKED).astype(jnp.float32)
            if turn < 3:
                rows = (k, v, q)[turn][pl.ds(b * BLOCK, BLOCK)]
                kvq[:, turn, b] = jnp.swapaxes(rows, 0, 1)
            return carry

        lax.fori_loop(0, NBD, query_block, 0, unroll=5)
    for g in range(G):
        enter_block(NR + g, gid[g])


def finish_kernel(dqh, dkh, dvh, summed, dq, dk, dv, projected):
    projected[...] = summed[...]
    for ref, out in ((dqh, dq), (dkh, dk), (dvh, dv)):
        out[...] = jnp.swapaxes(ref[...].reshape(HPD, HERE, HD), 0, 1)


def local(queries, key_rows, value_rows, out_weight, out_grad, global_ids, random_ids, random_count):
    bf16, f32 = jnp.bfloat16, jnp.float32
    kvq, aux, off = pl.pallas_call(
        prepare_kernel,
        out_shape=(
            struct(HPD, 3, NBD, BLOCK, HD),
            jax.ShapeDtypeStruct((LISTED + NR + G,), jnp.int32),
            jax.ShapeDtypeStruct((NR,), jnp.float32),
        ),
        in_specs=[SMEM] * 3 + [VMEM] * 3,
        out_specs=(VMEM, SMEM, SMEM),
        compiler_params=pltpu.CompilerParams(vmem_limit_bytes=LIMIT),
    )(random_ids.T, random_count, global_ids, key_rows, value_rows, queries)
    w = out_weight.reshape(HPD * HD, out_weight.shape[2])
    both = 2 * PIECES

    def vmem(*shape, dtype=bf16):
        return pltpu.VMEM(shape, dtype)

    def blocks(*count, dtype=bf16):
        return vmem(*count, BLOCK, HD, dtype=dtype)

    one = pltpu.SemaphoreType.DMA
    summed, dqh, dkh, dvh = pl.pallas_call(
        layer_kernel,
        out_shape=(struct(HERE, SHARD),) + (struct(HPD, NBD, BLOCK, HD),) * 3,
        in_specs=[SMEM, SMEM, ANY, ANY, ANY],
        out_specs=(VMEM, ANY, ANY, ANY),
        scratch_shapes=[
            blocks(NB + 2), blocks(NB + 2), blocks(4 * NBD), blocks(4 * NBD), blocks(4 * NBD), blocks(4 * NBD),
            vmem(4 * NBD, BLOCK, 8 * BLOCK),
            vmem(8, HERE, SHARD), vmem(HERE, SHARD, dtype=f32), blocks(HPD, NBD), vmem(*w.shape),
            blocks(NB + 2, dtype=f32), blocks(NB + 2, dtype=f32), blocks(G, dtype=f32), blocks(G, dtype=f32),
            blocks(NR + G + 1, dtype=f32), blocks(NR + G + 1, dtype=f32),
            blocks(HPD, NBD), vmem(4, HERE, SHARD), vmem(HERE, SHARD), vmem(2, HERE, SHARD),
            blocks(8, 2, NBD), blocks(8, 2, NBD), blocks(4, 2, NBD), blocks(4, 2, NBD), blocks(4, 2, NBD),
            sem(4, both), sem(4, both), sem(4), sem(4), sem(4, both), sem(4, both), sem(8, both), sem(8, both),
            sem(4), sem(4), sem(3, 4), sem(3, 4), sem(4), sem(4), one, one,
            sem(4), sem(4), sem(4), sem(4), sem(8, both), sem(8, both), sem(4, both), sem(4, both),
            sem(4, both), sem(4, both), sem(4), sem(4), sem(4), sem(4), sem(2, 4), sem(2, 4),
        ],
        compiler_params=pltpu.CompilerParams(
            collective_id=0, has_side_effects=True, vmem_limit_bytes=LIMIT
        ),
    )(aux, off, kvq, out_grad, w)
    *grads, projected = pl.pallas_call(
        finish_kernel,
        out_shape=(struct(HERE, HPD, HD),) * 3 + (struct(HERE, SHARD),),
        in_specs=[VMEM] * 4,
        out_specs=(VMEM,) * 4,
        compiler_params=pltpu.CompilerParams(vmem_limit_bytes=LIMIT),
    )(dqh, dkh, dvh, summed)
    return (projected, *grads)


def solution(mesh):
    placed = (
        P("ctx", "head", None),
        P("ctx", "head", None),
        P("ctx", "head", None),
        P("head", None, None),
        P("ctx", "head"),
        P(),
        P(),
        P(),
    )
    return jax.shard_map(
        local,
        mesh=mesh,
        in_specs=placed,
        out_specs=(
            P("ctx", "head"),
            P("ctx", "head", None),
            P("ctx", "head", None),
            P("ctx", "head", None),
        ),
        check_vma=False,
    )
```
